256 devices in a mesh: gx: 8 (over z_hi, core), gy: 4 (over x), gz: 8 (over z_lo, y).
Axes of the slice: x: 4, y: 4, z: 8 (z_hi: 4, z_lo: 2; z = z_hi * 2 + z_lo), core: 2. Of those that a mesh axis runs over, the one named last changes fastest.
Arguments:
- tokens: bfloat16 [1024, 8192], P('gy', ('gz', 'gx')), may hold values from -6 to 6
- gate_weight: bfloat16 [8192, 14336], P('gz', ('gx', 'gy')), may hold values from -0.0625 to 0.0625
- up_weight: bfloat16 [8192, 14336], P('gz', ('gx', 'gy')), may hold values from -0.0625 to 0.0625
- down_weight: bfloat16 [14336, 8192], P('gx', ('gz', 'gy')), may hold values from -0.046875 to 0.046875
- out_grad: bfloat16 [1024, 8192], P('gy', ('gz', 'gx')), may hold values from -6 to 6
Outputs:
- mixed: bfloat16 [1024, 8192], P('gy', ('gz', 'gx'))
- tokens_grad: bfloat16 [1024, 8192], P('gy', ('gz', 'gx'))
- gate_grad: bfloat16 [8192, 14336], P('gz', ('gx', 'gy'))
- up_grad: bfloat16 [8192, 14336], P('gz', ('gx', 'gy'))
- down_grad: bfloat16 [14336, 8192], P('gx', ('gz', 'gy'))
The draws below stay inside these ranges and needn't reach their ends.
All inputs are finite; a program needn't handle non-finite values.
Results may differ from the reference program's by a relative error of at most 0.0049.
Values may be sent and summed in bfloat16 or wider, within the bound.
No kernel may reach another device: no remote copies, remote signals or barrier semaphores. Data moves between devices by JAX's collectives and lax.ppermute only.
A program may use at most 128 MiB of HBM per device.

```python
import jax
import jax.numpy as jnp
from jax import lax

D = 8192
FF = 14336
TOKENS = 1024


def steps_of(rng, extent, shards, low, largest):
    loudness = 1.0
    for dim, parts in shards:
        steps = jax.random.uniform(jax.random.fold_in(jax.random.fold_in(rng, 6), dim), (parts,), jnp.float32, low / len(shards), largest / len(shards))
        loudness = loudness * jnp.repeat(jnp.exp(steps), extent[dim] // parts).reshape((-1,) + (1,) * (len(extent) - 1 - dim))
    return loudness


def bell_draw(stream_key, dims, spread, bound, split=(), dtype=jnp.bfloat16):
    loudness = steps_of(stream_key, dims, split, -0.22, 0.18) if split else 1.0
    drawn = jax.random.normal(stream_key, dims, jnp.float32) * spread * loudness
    return jnp.minimum(jnp.maximum(drawn, -bound), bound).astype(dtype)


def setup_inputs(seed: int = 0) -> dict:
    key_list = jax.random.split(jax.random.key(seed), 6)
    tokens = bell_draw(key_list[0], (TOKENS, D), 1.0, 6.0, ((0, 4), (1, 64)))
    gate_weight = bell_draw(key_list[1], (D, FF), D ** -0.5, 0.0625, ((0, 8), (1, 32)))
    up_weight = bell_draw(key_list[2], (D, FF), D ** -0.5, 0.0625, ((0, 8), (1, 32)))
    down_weight = bell_draw(key_list[3], (FF, D), FF ** -0.5, 0.046875, ((0, 8), (1, 32)))
    out_grad = bell_draw(key_list[4], (TOKENS, D), 1.0, 6.0, ((0, 4), (1, 64)))
    return dict(tokens=tokens, gate_weight=gate_weight, up_weight=up_weight, down_weight=down_weight, out_grad=out_grad)


def left_product(left, right):
    return lax.dot_general(left, right, (((0,), (0,)), ((), ())), preferred_element_type=jnp.float32).astype(jnp.bfloat16)


def reference(tokens, gate_weight, up_weight, down_weight, out_grad):
    gate = jnp.dot(tokens, gate_weight, preferred_element_type=jnp.float32)
    up = jnp.dot(tokens, up_weight, preferred_element_type=jnp.float32)
    sig = jax.nn.sigmoid(gate)
    act = gate * sig
    hidden = (act * up).astype(jnp.bfloat16)
    mixed = jnp.dot(hidden, down_weight, preferred_element_type=jnp.float32).astype(jnp.bfloat16)
    hidden_grad = lax.dot_general(out_grad, down_weight, (((1,), (1,)), ((), ())), preferred_element_type=jnp.float32)
    gate_delta = (hidden_grad * up * sig * (1.0 + gate * (1.0 - sig))).astype(jnp.bfloat16)
    up_delta = (hidden_grad * act).astype(jnp.bfloat16)
    tokens_grad = lax.dot_general(gate_delta, gate_weight, (((1,), (1,)), ((), ())), preferred_element_type=jnp.float32)
    tokens_grad = tokens_grad + lax.dot_general(up_delta, up_weight, (((1,), (1,)), ((), ())), preferred_element_type=jnp.float32)
    tokens_grad = tokens_grad.astype(jnp.bfloat16)
    gate_grad = left_product(tokens, gate_delta)
    up_grad = left_product(tokens, up_delta)
    down_grad = left_product(hidden, out_grad)
    return mixed, tokens_grad, gate_grad, up_grad, down_grad
```

```python
import functools

import jax
import jax.numpy as jnp
from jax import lax
from jax.experimental import pallas as pl
from jax.experimental.pallas import tpu as pltpu
from jax.sharding import PartitionSpec as P

F32 = jnp.float32
BF16 = jnp.bfloat16
VMEM_LIMIT = 48 * 1024 * 1024


def shift_hi(k):
    return [(h * 2 + c, (h + k) % 4 * 2 + c) for h in range(4) for c in range(2)]


def shift_x(k):
    return [(g, (g + k) % 4) for g in range(4)]


def shift_y(k):
    return [(z * 4 + y, z * 4 + (y + k) % 4) for z in range(2) for y in range(4)]


SWAP_CORE = [(i, i ^ 1) for i in range(8)]
SWAP_LO = [(i, i ^ 4) for i in range(8)]


def send(value, axis, moves):
    return lax.ppermute(value, axis, moves)


def call(kernel, outs, args, flops, scratch=()):
    moved = sum(a.size * a.dtype.itemsize for a in args) + sum(
        o.size * o.dtype.itemsize for o in outs
    )
    return pl.pallas_call(
        kernel,
        out_shape=outs,
        in_specs=[pl.BlockSpec(memory_space=pltpu.SMEM)]
        + [pl.BlockSpec(memory_space=pltpu.VMEM)] * (len(args) - 1),
        out_specs=[pl.BlockSpec(memory_space=pltpu.VMEM)] * len(outs),
        scratch_shapes=list(scratch),
        compiler_params=pltpu.CompilerParams(vmem_limit_bytes=VMEM_LIMIT),
        cost_estimate=pl.CostEstimate(flops=flops, bytes_accessed=moved, transcendentals=0),
    )(*args)


def shape(dims, dtype):
    return jax.ShapeDtypeStruct(dims, dtype)


def dot_nt(left, right):
    return lax.dot_general(left, right, (((1,), (1,)), ((), ())), preferred_element_type=F32)


def dot_tn(left, right):
    return lax.dot_general(left, right, (((0,), (0,)), ((), ())), preferred_element_type=F32)


def rows_of(start, size):
    return pl.ds(pl.multiple_of(start, size), size)


def place_activation(hi, core, own_ref, other_ref, act_ref):
    for k in range(4):
        block = lax.rem(hi + 4 - k, 4) * 2
        for x in range(4):
            rows = slice(x * 256, (x + 1) * 256)
            act_ref[rows, rows_of((block + core) * 128, 128)] = own_ref[x, k]
            act_ref[rows, rows_of((block + 1 - core) * 128, 128)] = other_ref[x, k]


def partials(y, weights, act_ref, keep_ref, sends):
    for k in (2, 1, 3, 0):
        act = act_ref[rows_of(lax.rem(y + k, 4) * 256, 256), :]
        for i, w_ref in enumerate(weights):
            part = dot_nt(w_ref[...], act)
            if k:
                sends[k - 1][i] = part.astype(BF16)
            else:
                keep_ref[i] = part


def first_kernel(idx, own, other, gate_w, up_w, act, keep, s1, s2, s3):
    place_activation(idx[0], idx[1], own, other, act)
    partials(idx[3], (gate_w, up_w), act, keep, (s1, s2, s3))


def second_kernel(idx, own, other, w0, w1, w2, w3, act, weight, keep, s1, s2, s3):
    for k, w in enumerate((w0, w1, w2, w3)):
        weight[:, rows_of(lax.rem(idx[2] + 4 - k, 4) * 256, 256)] = w[...]
    place_activation(idx[0], idx[1], own, other, act)
    partials(idx[3], (weight,), act, keep, (s1, s2, s3))


def back_kernel(n, idx, *refs):
    pieces, weights = refs[:4], refs[4 : 4 + n]
    whole, own, other = refs[4 + n : 7 + n]
    columns = refs[7 + n]
    hi, core, y, lo = idx[0], idx[1], idx[3], idx[4]
    for k, piece in enumerate(pieces):
        start = lax.rem(y + 4 - k, 4) * 256
        for j, half in ((0, lo), (1, 1 - lo)):
            for i in range(n):
                whole[i, :, rows_of(start + half * 128, 128)] = piece[j, i]
    for i, w in enumerate(weights):
        for k in range(4):
            block = lax.rem(hi + k, 4) * 2
            columns[1, i, :, k * 128 : (k + 1) * 128] = w[:, rows_of((block + core) * 128, 128)]
            columns[0, i, :, k * 128 : (k + 1) * 128] = w[:, rows_of((block + 1 - core) * 128, 128)]
    for side, out in ((0, other), (1, own)):
        for t in range(4):
            rows = slice(t * 256, (t + 1) * 256)
            total = dot_tn(whole[0, :, rows], columns[side, 0])
            for i in range(1, n):
                total = total + dot_tn(whole[i, :, rows], columns[side, i])
            out[rows, :] = total


def spread_x(block):
    return jnp.stack([block] + [send(block, "gy", shift_x(k)) for k in (1, 2, 3)])


def sum_y(keep, parts):
    total = keep
    for k, part in zip((1, 2, 3), parts):
        total = total + send(part, "gz", shift_y(k)).astype(F32)
    return total


def sum_rows(keep, parts, lo):
    total = sum_y(keep, parts)
    low, high = total[..., :128], total[..., 128:]
    mine = jnp.where(lo == 0, low, high)
    theirs = jnp.where(lo == 0, high, low)
    return mine + send(theirs, "gz", SWAP_LO)


def gather_rows(block):
    pair = jnp.stack([block, send(block, "gz", SWAP_LO)])
    return [pair] + [send(pair, "gz", shift_y(k)) for k in (1, 2, 3)]


def sum_columns(own, other):
    total = own + send(other, "gx", SWAP_CORE)
    rows = total[:256]
    for k in (1, 2, 3):
        rows = rows + send(
            total[k * 256 : (k + 1) * 256].astype(BF16), "gy", shift_x(-k)
        ).astype(F32)
    out = rows[:, :128]
    for k in (1, 2, 3):
        out = out + send(rows[:, k * 128 : (k + 1) * 128], "gx", shift_hi(k))
    return out.astype(BF16)


def local(tokens, gate_weight, up_weight, down_weight, out_grad):
    gx, gy, gz = lax.axis_index("gx"), lax.axis_index("gy"), lax.axis_index("gz")
    lo = gz // 4
    idx = jnp.stack([gx // 2, gx % 2, gy, gz % 4, lo]).astype(jnp.int32)
    gate_w, up_w = gate_weight.T, up_weight.T

    both = jnp.stack([tokens, out_grad])
    by_hi = [both] + [send(both, "gx", shift_hi(k)) for k in (1, 2, 3)]
    down = [
        lax.dynamic_slice(down_weight, (lax.rem(gy + k, 4) * 448, 0), (448, 256))
        for k in range(4)
    ]
    down = [down[0]] + [send(down[k], "gy", shift_x(k)) for k in (1, 2, 3)]
    tok_own = spread_x(jnp.stack([b[0] for b in by_hi]))
    tok_other = send(tok_own, "gx", SWAP_CORE)
    grad_own = spread_x(jnp.stack([b[1] for b in by_hi]))
    grad_other = send(grad_own, "gx", SWAP_CORE)

    msg = [shape((2, 448, 256), BF16)] * 3
    tok, gu_keep, *gu_parts = call(
        first_kernel,
        [shape((1024, 1024), BF16), shape((2, 448, 256), F32)] + msg,
        (idx, tok_own, tok_other, gate_w, up_w),
        4 * 1024 * 1024 * 448,
    )
    msg = [shape((1, 448, 256), BF16)] * 3
    grad, down_w, dh_keep, *dh_parts = call(
        second_kernel,
        [shape((1024, 1024), BF16), shape((448, 1024), BF16), shape((1, 448, 256), F32)] + msg,
        (idx, grad_own, grad_other, *down),
        2 * 1024 * 1024 * 448,
    )
    gate_up = sum_rows(gu_keep, gu_parts, lo)
    dh = sum_rows(dh_keep, dh_parts, lo)[0]
    gate, up = gate_up[0], gate_up[1]
    sig = jax.nn.sigmoid(gate)
    act = gate * sig
    hidden = (act * up).astype(BF16)
    gate_delta = (dh * up * sig * (1.0 + gate * (1.0 - sig))).astype(BF16)
    up_delta = (dh * act).astype(BF16)

    hid, mixed_own, mixed_other = call(
        functools.partial(back_kernel, 1),
        [shape((1, 448, 1024), BF16), shape((1024, 512), F32), shape((1024, 512), F32)],
        (idx, *gather_rows(hidden[None]), down_w),
        2 * 1024 * 1024 * 448,
        [pltpu.VMEM((2, 1, 448, 512), BF16)],
    )
    mixed = sum_columns(mixed_own, mixed_other)
    delta, dx_own, dx_other = call(
        functools.partial(back_kernel, 2),
        [shape((2, 448, 1024), BF16), shape((1024, 512), F32), shape((1024, 512), F32)],
        (idx, *gather_rows(jnp.stack([gate_delta, up_delta])), gate_w, up_w),
        4 * 1024 * 1024 * 448,
        [pltpu.VMEM((2, 2, 448, 512), BF16)],
    )
    tokens_grad = sum_columns(dx_own, dx_other)

    product = jnp.dot(hid[0], grad, preferred_element_type=F32).astype(BF16)
    pieces = [
        lax.dynamic_slice(product, (0, lax.rem(gy + k, 4) * 256), (448, 256)) for k in range(4)
    ]
    down_grad = jnp.zeros((1792, 256), BF16)
    for k in range(4):
        piece = send(pieces[k], "gy", shift_x(k)) if k else pieces[0]
        down_grad = lax.dynamic_update_slice(down_grad, piece, (lax.rem(gy + 4 - k, 4) * 448, 0))
    gate_grad = jnp.dot(delta[0], tok, preferred_element_type=F32).astype(BF16).T
    up_grad = jnp.dot(delta[1], tok, preferred_element_type=F32).astype(BF16).T
    return mixed, tokens_grad, gate_grad, up_grad, down_grad


def solution(mesh):
    in_specs = (
        P("gy", ("gz", "gx")),
        P("gz", ("gx", "gy")),
        P("gz", ("gx", "gy")),
        P("gx", ("gz", "gy")),
        P("gy", ("gz", "gx")),
    )
    out_specs = (
        P("gy", ("gz", "gx")),
        P("gy", ("gz", "gx")),
        P("gz", ("gx", "gy")),
        P("gz", ("gx", "gy")),
        P("gx", ("gz", "gy")),
    )
    return jax.shard_map(local, mesh=mesh, in_specs=in_specs, out_specs=out_specs, check_vma=False)
```

```python
import functools

import jax
import jax.numpy as jnp
from jax import lax
from jax.experimental import pallas as pl
from jax.experimental.pallas import tpu as pltpu
from jax.sharding import PartitionSpec as P

F32 = jnp.float32
BF16 = jnp.bfloat16
VMEM_LIMIT = 24 * 1024 * 1024


def shift_hi(k):
    return [(h * 2 + c, (h + k) % 4 * 2 + c) for h in range(4) for c in range(2)]


def shift_x(k):
    return [(g, (g + k) % 4) for g in range(4)]


def shift_y(k):
    return [(z * 4 + y, z * 4 + (y + k) % 4) for z in range(2) for y in range(4)]


SWAP_CORE = [(i, i ^ 1) for i in range(8)]
SWAP_LO = [(i, i ^ 4) for i in range(8)]


def send(value, axis, moves):
    return lax.ppermute(value, axis, moves)


def staged(kernel, n_in, outs, far, n_scratch):
    n_out = len(outs)

    def run(idx, *refs):
        inputs, results = refs[:n_in], refs[n_in : n_in + n_out]
        scratch = refs[n_in + n_out : n_in + n_out + n_scratch]
        held = refs[n_in + n_out + n_scratch : -1]
        held, near, sems = held[:n_in], held[n_in:], refs[-1]
        copies = [
            pltpu.make_async_copy(src, dst, sems.at[i])
            for i, (src, dst) in enumerate(zip(inputs, held))
        ]
        for copy in copies:
            copy.start()
        for copy in copies:
            copy.wait()
        local_results = list(results)
        for i, ref in zip(far, near):
            local_results[i] = ref
        kernel(idx, *held, *local_results, *scratch)
        copies = [
            pltpu.make_async_copy(ref, results[i], sems.at[n_in + n])
            for n, (i, ref) in enumerate(zip(far, near))
        ]
        for copy in copies:
            copy.start()
        for copy in copies:
            copy.wait()

    return run


def call(kernel, outs, args, far_in=(), far=(), scratch=()):
    n = len(args) - 1
    return pl.pallas_call(
        staged(kernel, n, outs, far, len(scratch)),
        out_shape=[
            pltpu.HBM(o.shape, o.dtype) if i in far else o for i, o in enumerate(outs)
        ],
        in_specs=[pl.BlockSpec(memory_space=pltpu.SMEM)]
        + [pl.BlockSpec(memory_space=pltpu.HBM if i in far_in else pl.ANY) for i in range(n)],
        out_specs=[
            pl.BlockSpec(memory_space=pltpu.HBM if i in far else pltpu.VMEM)
            for i in range(len(outs))
        ],
        scratch_shapes=list(scratch)
        + [pltpu.VMEM(a.shape, a.dtype) for a in args[1:]]
        + [pltpu.VMEM(outs[i].shape, outs[i].dtype) for i in far]
        + [pltpu.SemaphoreType.DMA((n + len(far),))],
        compiler_params=pltpu.CompilerParams(vmem_limit_bytes=VMEM_LIMIT),
        cost_estimate=pl.CostEstimate(flops=1, bytes_accessed=1, transcendentals=0),
    )(
        args[0],
        *[
            pltpu.with_memory_space_constraint(a, pltpu.HBM) if i in far_in else a
            for i, a in enumerate(args[1:])
        ],
    )


def shape(dims, dtype):
    return jax.ShapeDtypeStruct(dims, dtype)


def dot_nt(left, right):
    return lax.dot_general(left, right, (((1,), (1,)), ((), ())), preferred_element_type=F32)


def dot_tn(left, right):
    return lax.dot_general(left, right, (((0,), (0,)), ((), ())), preferred_element_type=F32)


def rows_of(start, size):
    return pl.ds(pl.multiple_of(start, size), size)


def place_activation(hi, core, own_ref, other_ref, act_ref):
    for k in range(4):
        block = lax.rem(hi + 4 - k, 4) * 2
        for x in range(4):
            rows = slice(x * 256, (x + 1) * 256)
            act_ref[rows, rows_of((block + core) * 128, 128)] = own_ref[x, k]
            act_ref[rows, rows_of((block + 1 - core) * 128, 128)] = other_ref[x, k]


def partials(y, weights, act_ref, sends):
    for k in (2, 1, 3):
        act = act_ref[rows_of(lax.rem(y + k, 4) * 256, 256), :]
        for i, w_ref in enumerate(weights):
            sends[k - 1][i] = dot_nt(w_ref[...], act).astype(BF16)


def kept(y, weights, act_ref, keep_ref):
    act = act_ref[rows_of(y * 256, 256), :]
    for i, w_ref in enumerate(weights):
        keep_ref[i] = dot_nt(w_ref[...], act)


def first_kernel(idx, own, other, gate_w, up_w, act, s1, s2, s3):
    place_activation(idx[0], idx[1], own, other, act)
    partials(idx[3], (gate_w, up_w), act, (s1, s2, s3))


def keep_kernel(idx, act, gate_w, up_w, keep):
    kept(idx[3], (gate_w, up_w), act, keep)


def second_kernel(idx, blocks, down, act, weight, keep, s1, s2, s3):
    for x in range(4):
        weight[:, x * 256 : (x + 1) * 256] = down[x]
    for k in range(4):
        x = lax.rem(idx[2] + 4 - k, 4)
        for b in range(8):
            act[k * 256 : (k + 1) * 256, b * 128 : (b + 1) * 128] = blocks[b * 4 + x]
    partials(idx[3], (weight,), act, (s1, s2, s3))
    kept(idx[3], (weight,), act, keep)


def back_kernel(n, idx, *refs):
    pieces, weights = refs[:4], refs[4 : 4 + n]
    whole, own, other = refs[4 + n : 7 + n]
    columns = refs[7 + n]
    hi, core, y, lo = idx[0], idx[1], idx[3], idx[4]
    for k, piece in enumerate(pieces):
        start = lax.rem(y + 4 - k, 4) * 256
        for j, half in ((0, lo), (1, 1 - lo)):
            for i in range(n):
                whole[i, :, rows_of(start + half * 128, 128)] = piece[j, i]
    for i, w in enumerate(weights):
        for k in range(4):
            block = lax.rem(hi + k, 4) * 2
            columns[1, i, :, k * 128 : (k + 1) * 128] = w[:, rows_of((block + core) * 128, 128)]
            columns[0, i, :, k * 128 : (k + 1) * 128] = w[:, rows_of((block + 1 - core) * 128, 128)]
    for side, out in ((0, other), (1, own)):
        for t in range(4):
            rows = slice(t * 256, (t + 1) * 256)
            total = dot_tn(whole[0, :, rows], columns[side, 0])
            for i in range(1, n):
                total = total + dot_tn(whole[i, :, rows], columns[side, i])
            out[rows, :] = total


def product_kernel(idx, hid, grad, out):
    for x in range(4):
        part = jnp.dot(hid[0], grad[:, x * 256 : (x + 1) * 256], preferred_element_type=F32)
        out[x] = part.astype(BF16)


def exchange_x(blocks):
    return lax.all_to_all(blocks, "gy", split_axis=0, concat_axis=0, tiled=True)


def together(values):
    return list(lax.optimization_barrier(tuple(values)))


def after(value, *others):
    return lax.optimization_barrier((value, others))[0]


def spread_x(block):
    return [block] + together([send(block, "gy", shift_x(k)) for k in (1, 2, 3)])


def send_y(parts):
    return together([send(part, "gz", shift_y(k)) for k, part in zip((1, 2, 3), parts)])


def sum_rows(keep, received, lo):
    total = keep
    for part in received:
        total = total + part.astype(F32)
    low, high = total[..., :128], total[..., 128:]
    mine = jnp.where(lo == 0, low, high)
    theirs = jnp.where(lo == 0, high, low)
    return mine + send(theirs, "gz", SWAP_LO)


def pair_rows(block):
    return jnp.stack([block, send(block, "gz", SWAP_LO)])


def spread_y(pair):
    return [pair] + together([send(pair, "gz", shift_y(k)) for k in (1, 2, 3)])


def sum_core(own, other):
    total = own + send(other, "gx", SWAP_CORE)
    return total[:256], [total[k * 256 : (k + 1) * 256].astype(BF16) for k in (1, 2, 3)]


def send_x(parts):
    return together([send(part, "gy", shift_x(-k)) for k, part in zip((1, 2, 3), parts)])


def sum_x(rows, received):
    for part in received:
        rows = rows + part.astype(F32)
    return rows


def sum_columns_hi(rows):
    out = rows[:, :128]
    parts = [rows[:, k * 128 : (k + 1) * 128].astype(BF16) for k in (1, 2, 3)]
    for part in together([send(p, "gx", shift_hi(k)) for k, p in zip((1, 2, 3), parts)]):
        out = out + part.astype(F32)
    return out.astype(BF16)


def local(tokens, gate_weight, up_weight, down_weight, out_grad):
    gx, gy, gz = lax.axis_index("gx"), lax.axis_index("gy"), lax.axis_index("gz")
    lo = gz // 4
    idx = jnp.stack([gx // 2, gx % 2, gy, gz % 4, lo]).astype(jnp.int32)
    gate_w, up_w = gate_weight.T, up_weight.T

    grad_blocks = lax.all_gather(out_grad, ("gx", "gy"), axis=0)
    by_hi = [tokens] + together([send(tokens, "gx", shift_hi(k)) for k in (1, 2, 3)])
    down = exchange_x(down_weight.reshape(4, 448, 256))
    tok_own = jnp.stack(after(spread_x(jnp.stack(by_hi)), down))
    tok_other = send(tok_own, "gx", SWAP_CORE)

    msg = [shape((2, 448, 256), BF16)] * 3
    tok, *gu_parts = call(
        first_kernel,
        [shape((1024, 1024), BF16)] + msg,
        (idx, tok_own, tok_other, gate_w, up_w),
        (2, 3),
        (0,),
    )
    gu_received = send_y(gu_parts)
    (gu_keep,) = call(
        keep_kernel,
        [shape((2, 448, 256), F32)],
        (idx, tok, gate_w, up_w),
        (0, 1, 2),
    )
    msg = [shape((1, 448, 256), BF16)] * 3
    grad, down_w, dh_keep, *dh_parts = call(
        second_kernel,
        [shape((1024, 1024), BF16), shape((448, 1024), BF16), shape((1, 448, 256), F32)] + msg,
        (idx, grad_blocks, down),
        (0, 1),
        (0, 1),
    )
    gu_received, dh_parts = lax.optimization_barrier((gu_received, dh_parts))
    gate_up = sum_rows(gu_keep, gu_received, lo)
    dh = sum_rows(dh_keep, send_y(dh_parts), lo)[0]
    gate, up = gate_up[0], gate_up[1]
    sig = jax.nn.sigmoid(gate)
    act = gate * sig
    hidden = (act * up).astype(BF16)
    gate_delta = (dh * up * sig * (1.0 + gate * (1.0 - sig))).astype(BF16)
    up_delta = (dh * act).astype(BF16)

    hid_pair = pair_rows(hidden[None])
    hid_pieces = spread_y(hid_pair)
    delta_pair = pair_rows(after(jnp.stack([gate_delta, up_delta]), hid_pair))
    delta_pieces = spread_y(after(delta_pair, *hid_pieces[1:]))
    hid_pieces = after(hid_pieces, delta_pair)
    hid, mixed_own, mixed_other = call(
        functools.partial(back_kernel, 1),
        [shape((1, 448, 1024), BF16), shape((1024, 512), F32), shape((1024, 512), F32)],
        (idx, *hid_pieces, down_w),
        (4,),
        (0,),
        [pltpu.VMEM((2, 1, 448, 512), BF16)],
    )
    mixed_rows, mixed_parts = sum_core(mixed_own, mixed_other)
    mixed_received = send_x(mixed_parts)
    mixed_rows = sum_x(mixed_rows, mixed_received)
    (product,) = call(
        product_kernel,
        [shape((4, 448, 256), BF16)],
        (idx, hid, grad),
        (0, 1),
    )
    down_grad = exchange_x(product).reshape(1792, 256)
    delta_pieces = after(delta_pieces, mixed_received, down_grad)
    delta, dx_own, dx_other = call(
        functools.partial(back_kernel, 2),
        [shape((2, 448, 1024), BF16), shape((1024, 512), F32), shape((1024, 512), F32)],
        (idx, *delta_pieces, gate_w, up_w),
        (4, 5),
        (0,),
        [pltpu.VMEM((2, 2, 448, 512), BF16)],
    )
    dx_rows, dx_parts = sum_core(dx_own, dx_other)
    mixed = sum_columns_hi(after(mixed_rows, dx_parts))
    tokens_grad = sum_columns_hi(sum_x(dx_rows, send_x(dx_parts)))

    gate_grad = jnp.dot(delta[0], tok, preferred_element_type=F32).astype(BF16).T
    up_grad = jnp.dot(delta[1], tok, preferred_element_type=F32).astype(BF16).T
    return mixed, tokens_grad, gate_grad, up_grad, down_grad


def solution(mesh):
    in_specs = (
        P("gy", ("gz", "gx")),
        P("gz", ("gx", "gy")),
        P("gz", ("gx", "gy")),
        P("gx", ("gz", "gy")),
        P("gy", ("gz", "gx")),
    )
    out_specs = (
        P("gy", ("gz", "gx")),
        P("gy", ("gz", "gx")),
        P("gz", ("gx", "gy")),
        P("gz", ("gx", "gy")),
        P("gx", ("gz", "gy")),
    )
    return jax.shard_map(local, mesh=mesh, in_specs=in_specs, out_specs=out_specs, check_vma=False)
```

```python
import functools

import jax
import jax.numpy as jnp
from jax import lax
from jax.experimental import pallas as pl
from jax.experimental.pallas import tpu as pltpu
from jax.sharding import PartitionSpec as P

F32 = jnp.float32
BF16 = jnp.bfloat16
VMEM_LIMIT = 24 * 1024 * 1024


def shift_x(k):
    return [(g, (g + k) % 4) for g in range(4)]


def shift_y(k):
    return [(z * 4 + y, z * 4 + (y + k) % 4) for z in range(2) for y in range(4)]


SWAP_CORE = [(i, i ^ 1) for i in range(8)]
SWAP_LO = [(i, i ^ 4) for i in range(8)]
SWAP_HI_NEAR = [(i, i ^ 2) for i in range(8)]
SWAP_HI_FAR = [(i, i ^ 6) for i in range(8)]


def send(value, axis, moves):
    return lax.ppermute(value, axis, moves)


def staged(kernel, n_in, outs, far, n_scratch):
    n_out = len(outs)

    def run(idx, *refs):
        inputs, results = refs[:n_in], refs[n_in : n_in + n_out]
        scratch = refs[n_in + n_out : n_in + n_out + n_scratch]
        held = refs[n_in + n_out + n_scratch : -1]
        held, near, sems = held[:n_in], held[n_in:], refs[-1]
        copies = [
            pltpu.make_async_copy(src, dst, sems.at[i])
            for i, (src, dst) in enumerate(zip(inputs, held))
        ]
        for copy in copies:
            copy.start()
        for copy in copies:
            copy.wait()
        local_results = list(results)
        for i, ref in zip(far, near):
            local_results[i] = ref
        kernel(idx, *held, *local_results, *scratch)
        copies = [
            pltpu.make_async_copy(ref, results[i], sems.at[n_in + n])
            for n, (i, ref) in enumerate(zip(far, near))
        ]
        for copy in copies:
            copy.start()
        for copy in copies:
            copy.wait()

    return run


def call(kernel, outs, args, far_in=(), far=(), scratch=()):
    n = len(args) - 1
    return pl.pallas_call(
        staged(kernel, n, outs, far, len(scratch)),
        out_shape=[
            pltpu.HBM(o.shape, o.dtype) if i in far else o for i, o in enumerate(outs)
        ],
        in_specs=[pl.BlockSpec(memory_space=pltpu.SMEM)]
        + [pl.BlockSpec(memory_space=pltpu.HBM if i in far_in else pl.ANY) for i in range(n)],
        out_specs=[
            pl.BlockSpec(memory_space=pltpu.HBM if i in far else pltpu.VMEM)
            for i in range(len(outs))
        ],
        scratch_shapes=list(scratch)
        + [pltpu.VMEM(a.shape, a.dtype) for a in args[1:]]
        + [pltpu.VMEM(outs[i].shape, outs[i].dtype) for i in far]
        + [pltpu.SemaphoreType.DMA((n + len(far),))],
        compiler_params=pltpu.CompilerParams(vmem_limit_bytes=VMEM_LIMIT),
        cost_estimate=pl.CostEstimate(flops=1, bytes_accessed=1, transcendentals=0),
    )(
        args[0],
        *[
            pltpu.with_memory_space_constraint(a, pltpu.HBM) if i in far_in else a
            for i, a in enumerate(args[1:])
        ],
    )


def shape(dims, dtype):
    return jax.ShapeDtypeStruct(dims, dtype)


def dot_nt(left, right):
    return lax.dot_general(left, right, (((1,), (1,)), ((), ())), preferred_element_type=F32)


def dot_tn(left, right):
    return lax.dot_general(left, right, (((0,), (0,)), ((), ())), preferred_element_type=F32)


def rows_of(start, size):
    return pl.ds(pl.multiple_of(start, size), size)


GATHERED = (0, 1, 3, 2)
SCATTERED = (0, 3, 1, 2)


def place_activation(hi, core, own_ref, other_ref, act_ref, order):
    for slot, mask in enumerate(GATHERED):
        block = (hi ^ mask) * 2
        for x in range(4):
            rows = slice(x * 256, (x + 1) * 256)
            act_ref[rows, rows_of((block + core) * 128, 128)] = own_ref[order[x], slot]
            act_ref[rows, rows_of((block + 1 - core) * 128, 128)] = other_ref[order[x], slot]


def partials(y, weights, act_ref, sends):
    for k in (2, 1, 3):
        act = act_ref[rows_of(lax.rem(y + k, 4) * 256, 256), :]
        for i, w_ref in enumerate(weights):
            sends[k - 1][i] = dot_nt(w_ref[...], act).astype(BF16)


def kept(y, weights, act_ref, keep_ref):
    act = act_ref[rows_of(y * 256, 256), :]
    for i, w_ref in enumerate(weights):
        keep_ref[i] = dot_nt(w_ref[...], act)


def first_kernel(idx, own, other, gate_w, up_w, act, s1, s2, s3):
    place_activation(idx[0], idx[1], own, other, act, range(4))
    partials(idx[3], (gate_w, up_w), act, (s1, s2, s3))


def keep_kernel(idx, act, gate_w, up_w, keep):
    kept(idx[3], (gate_w, up_w), act, keep)


def second_kernel(idx, own, other, down, act, weight, keep, s1, s2, s3):
    for x in range(4):
        weight[:, x * 256 : (x + 1) * 256] = down[x]
    order = [lax.rem(idx[2] + 4 - k, 4) for k in range(4)]
    place_activation(idx[0], idx[1], own, other, act, order)
    partials(idx[3], (weight,), act, (s1, s2, s3))
    kept(idx[3], (weight,), act, keep)


def back_kernel(n, idx, *refs):
    pieces, weights = refs[:4], refs[4 : 4 + n]
    whole, own, other = refs[4 + n : 7 + n]
    columns = refs[7 + n]
    hi, core, y, lo = idx[0], idx[1], idx[3], idx[4]
    for k, piece in enumerate(pieces):
        start = lax.rem(y + 4 - k, 4) * 256
        for j, half in ((0, lo), (1, 1 - lo)):
            for i in range(n):
                whole[i, :, rows_of(start + half * 128, 128)] = piece[j, i]
    for i, w in enumerate(weights):
        for k, mask in enumerate(SCATTERED):
            block = (hi ^ mask) * 2
            columns[1, i, :, k * 128 : (k + 1) * 128] = w[:, rows_of((block + core) * 128, 128)]
            columns[0, i, :, k * 128 : (k + 1) * 128] = w[:, rows_of((block + 1 - core) * 128, 128)]
    for side, out in ((0, other), (1, own)):
        for t in range(4):
            rows = slice(t * 256, (t + 1) * 256)
            total = dot_tn(whole[0, :, rows], columns[side, 0])
            for i in range(1, n):
                total = total + dot_tn(whole[i, :, rows], columns[side, i])
            out[rows, :] = total


def product_kernel(idx, hid, grad, out):
    for x in range(4):
        part = jnp.dot(hid[0], grad[:, x * 256 : (x + 1) * 256], preferred_element_type=F32)
        out[x] = part.astype(BF16)


def exchange_x(blocks):
    return lax.all_to_all(blocks, "gy", split_axis=0, concat_axis=0, tiled=True)


def together(values):
    return list(lax.optimization_barrier(tuple(values)))


def after(value, *others):
    return lax.optimization_barrier((value, others))[0]


def spread_x(block):
    return [block] + together([send(block, "gy", shift_x(k)) for k in (1, 2, 3)])


def send_y(parts):
    return together([send(part, "gz", shift_y(k)) for k, part in zip((1, 2, 3), parts)])


def sum_rows(keep, received, lo):
    total = keep
    for part in received:
        total = total + part.astype(F32)
    low, high = total[..., :128], total[..., 128:]
    mine = jnp.where(lo == 0, low, high)
    theirs = jnp.where(lo == 0, high, low)
    return mine + send(theirs, "gz", SWAP_LO)


def pair_rows(block):
    return jnp.stack([block, send(block, "gz", SWAP_LO)])


def spread_y(pair):
    return [pair] + together([send(pair, "gz", shift_y(k)) for k in (1, 2, 3)])


def sum_core(own, other):
    total = own + send(other, "gx", SWAP_CORE)
    return total[:256], [total[k * 256 : (k + 1) * 256].astype(BF16) for k in (1, 2, 3)]


def send_x(parts):
    return together([send(part, "gy", shift_x(-k)) for k, part in zip((1, 2, 3), parts)])


def sum_x(rows, received):
    for part in received:
        rows = rows + part.astype(F32)
    return rows


def gather_hi(block):
    pair = jnp.stack([block, send(block, "gx", SWAP_HI_NEAR)])
    return jnp.concatenate([pair, send(pair, "gx", SWAP_HI_FAR)])


def sum_columns_hi(rows):
    near = send(rows[:, 256:].astype(BF16), "gx", SWAP_HI_NEAR)
    rows = rows[:, :256] + near.astype(F32)
    far = send(rows[:, 128:].astype(BF16), "gx", SWAP_HI_FAR)
    return (rows[:, :128] + far.astype(F32)).astype(BF16)


def local(tokens, gate_weight, up_weight, down_weight, out_grad):
    gx, gy, gz = lax.axis_index("gx"), lax.axis_index("gy"), lax.axis_index("gz")
    lo = gz // 4
    idx = jnp.stack([gx // 2, gx % 2, gy, gz % 4, lo]).astype(jnp.int32)
    gate_w, up_w = gate_weight.T, up_weight.T

    down = exchange_x(down_weight.reshape(4, 448, 256))
    tok_hi = gather_hi(tokens)
    tok_blocks = spread_x(tok_hi)
    grad_hi = gather_hi(after(out_grad, tok_hi))
    tok_own = jnp.stack(after(tok_blocks, down, grad_hi))
    tok_other = send(tok_own, "gx", SWAP_CORE)
    grad_own = exchange_x(jnp.broadcast_to(after(grad_hi, tok_own), (4, 4, 256, 128)))
    msg = [shape((2, 448, 256), BF16)] * 3
    tok, *gu_parts = call(
        first_kernel,
        [shape((1024, 1024), BF16)] + msg,
        (idx, tok_own, tok_other, gate_w, up_w),
        (2, 3),
        (0, 1, 2, 3),
    )
    gu_received = send_y(gu_parts)
    (gu_keep,) = call(
        keep_kernel,
        [shape((2, 448, 256), F32)],
        (idx, tok, gate_w, up_w),
        (0, 1, 2),
    )
    grad_other = send(after(grad_own, gu_received), "gx", SWAP_CORE)
    msg = [shape((1, 448, 256), BF16)] * 3
    grad, down_w, dh_keep, *dh_parts = call(
        second_kernel,
        [shape((1024, 1024), BF16), shape((448, 1024), BF16), shape((1, 448, 256), F32)] + msg,
        (idx, grad_own, grad_other, down),
        (2,),
        (0, 1),
    )
    gate_up = sum_rows(gu_keep, gu_received, lo)
    dh = sum_rows(dh_keep, send_y(dh_parts), lo)[0]
    gate, up = gate_up[0], gate_up[1]
    sig = jax.nn.sigmoid(gate)
    act = gate * sig
    hidden = (act * up).astype(BF16)
    gate_delta = (dh * up * sig * (1.0 + gate * (1.0 - sig))).astype(BF16)
    up_delta = (dh * act).astype(BF16)

    hid_pair = pair_rows(hidden[None])
    hid_pieces = spread_y(hid_pair)
    delta_pair = pair_rows(after(jnp.stack([gate_delta, up_delta]), hid_pair))
    delta_pieces = spread_y(delta_pair)
    hid_pieces = after(hid_pieces, delta_pair)
    hid, mixed_own, mixed_other = call(
        functools.partial(back_kernel, 1),
        [shape((1, 448, 1024), BF16), shape((1024, 512), F32), shape((1024, 512), F32)],
        (idx, *hid_pieces, down_w),
        (4,),
        (0,),
        [pltpu.VMEM((2, 1, 448, 512), BF16)],
    )
    mixed_rows, mixed_parts = sum_core(mixed_own, mixed_other)
    mixed_received = send_x(mixed_parts)
    mixed_rows = sum_x(mixed_rows, mixed_received)
    (product,) = call(
        product_kernel,
        [shape((4, 448, 256), BF16)],
        (idx, after(hid, mixed_parts), grad),
        (0, 1),
    )
    down_grad = exchange_x(product).reshape(1792, 256)
    delta_pieces = after(delta_pieces, mixed_received, product)
    delta, dx_own, dx_other = call(
        functools.partial(back_kernel, 2),
        [shape((2, 448, 1024), BF16), shape((1024, 512), F32), shape((1024, 512), F32)],
        (idx, *delta_pieces, gate_w, up_w),
        (4, 5),
        (0,),
        [pltpu.VMEM((2, 2, 448, 512), BF16)],
    )
    dx_rows, dx_parts = sum_core(dx_own, dx_other)
    delta = after(delta, dx_parts)
    mixed = sum_columns_hi(after(mixed_rows, dx_parts))
    dx_received = send_x(dx_parts)
    down_grad = after(down_grad, dx_received)
    tokens_grad = sum_columns_hi(sum_x(dx_rows, dx_received))

    gate_grad = jnp.dot(delta[0], tok, preferred_element_type=F32).astype(BF16).T
    up_grad = jnp.dot(delta[1], tok, preferred_element_type=F32).astype(BF16).T
    return mixed, tokens_grad, gate_grad, up_grad, down_grad


def solution(mesh):
    in_specs = (
        P("gy", ("gz", "gx")),
        P("gz", ("gx", "gy")),
        P("gz", ("gx", "gy")),
        P("gx", ("gz", "gy")),
        P("gy", ("gz", "gx")),
    )
    out_specs = (
        P("gy", ("gz", "gx")),
        P("gy", ("gz", "gx")),
        P("gz", ("gx", "gy")),
        P("gz", ("gx", "gy")),
        P("gx", ("gz", "gy")),
    )
    return jax.shard_map(local, mesh=mesh, in_specs=in_specs, out_specs=out_specs, check_vma=False)
```

```python
import jax
import jax.numpy as jnp
from jax import lax
from jax.experimental import pallas as pl
from jax.experimental.pallas import tpu as pltpu
from jax.sharding import PartitionSpec as P

F32 = jnp.float32
BF16 = jnp.bfloat16
VMEM_LIMIT = 24 * 1024 * 1024


def shift_x(k):
    return [(g, (g + k) % 4) for g in range(4)]


def shift_y(k):
    return [(z * 4 + y, z * 4 + (y + k) % 4) for z in range(2) for y in range(4)]


SWAP_CORE = [(i, i ^ 1) for i in range(8)]
SWAP_LO = [(i, i ^ 4) for i in range(8)]
SWAP_HI_NEAR = [(i, i ^ 2) for i in range(8)]
SWAP_HI_FAR = [(i, i ^ 6) for i in range(8)]


def send(value, axis, moves):
    return lax.ppermute(value, axis, moves)


def staged(kernel, n_in, outs, far, n_scratch):
    n_out = len(outs)

    def run(idx, *refs):
        inputs, results = refs[:n_in], refs[n_in : n_in + n_out]
        scratch = refs[n_in + n_out : n_in + n_out + n_scratch]
        held = refs[n_in + n_out + n_scratch : -1]
        held, near, sems = held[:n_in], held[n_in:], refs[-1]
        copies = [
            pltpu.make_async_copy(src, dst, sems.at[i])
            for i, (src, dst) in enumerate(zip(inputs, held))
        ]
        for copy in copies:
            copy.start()
        for copy in copies:
            copy.wait()
        local_results = list(results)
        for i, ref in zip(far, near):
            local_results[i] = ref
        leaving = {
            i: pltpu.make_async_copy(ref, results[i], sems.at[n_in + n])
            for n, (i, ref) in enumerate(zip(far, near))
        }
        kernel(lambda i: leaving[i].start(), idx, *held, *local_results, *scratch)
        for i in far:
            leaving[i].wait()

    return run


def call(kernel, outs, args, far_in=(), far=(), scratch=()):
    n = len(args) - 1
    return pl.pallas_call(
        staged(kernel, n, outs, far, len(scratch)),
        out_shape=[
            pltpu.HBM(o.shape, o.dtype) if i in far else o for i, o in enumerate(outs)
        ],
        in_specs=[pl.BlockSpec(memory_space=pltpu.SMEM)]
        + [pl.BlockSpec(memory_space=pltpu.HBM if i in far_in else pl.ANY) for i in range(n)],
        out_specs=[
            pl.BlockSpec(memory_space=pltpu.HBM if i in far else pltpu.VMEM)
            for i in range(len(outs))
        ],
        scratch_shapes=list(scratch)
        + [pltpu.VMEM(a.shape, a.dtype) for a in args[1:]]
        + [pltpu.VMEM(outs[i].shape, outs[i].dtype) for i in far]
        + [pltpu.SemaphoreType.DMA((n + len(far),))],
        compiler_params=pltpu.CompilerParams(vmem_limit_bytes=VMEM_LIMIT),
        cost_estimate=pl.CostEstimate(flops=1, bytes_accessed=1, transcendentals=0),
    )(
        args[0],
        *[
            pltpu.with_memory_space_constraint(a, pltpu.HBM) if i in far_in else a
            for i, a in enumerate(args[1:])
        ],
    )


def shape(dims, dtype):
    return jax.ShapeDtypeStruct(dims, dtype)


def dot_nt(left, right):
    return lax.dot_general(left, right, (((1,), (1,)), ((), ())), preferred_element_type=F32)


def dot_tn(left, right):
    return lax.dot_general(left, right, (((0,), (0,)), ((), ())), preferred_element_type=F32)


def rows_of(start, size):
    return pl.ds(pl.multiple_of(start, size), size)


GATHERED = (0, 1, 3, 2)
SCATTERED = (0, 3, 1, 2)


def place_activation(hi, core, own_ref, other_ref, act_ref, order):
    for slot, mask in enumerate(GATHERED):
        block = (hi ^ mask) * 2
        for x in range(4):
            rows = slice(x * 256, (x + 1) * 256)
            act_ref[rows, rows_of((block + core) * 128, 128)] = own_ref[order[x], slot]
            act_ref[rows, rows_of((block + 1 - core) * 128, 128)] = other_ref[order[x], slot]


def partials(y, weights, act_ref, sends, sent):
    for k in (2, 1, 3):
        act = act_ref[rows_of(lax.rem(y + k, 4) * 256, 256), :]
        for i, w_ref in enumerate(weights):
            sends[k - 1][i] = dot_nt(w_ref[...], act).astype(BF16)
        sent(k)


def kept(y, weights, act_ref, keep_ref):
    act = act_ref[rows_of(y * 256, 256), :]
    for i, w_ref in enumerate(weights):
        keep_ref[i] = dot_nt(w_ref[...], act)


def first_kernel(flush, idx, own, other, gate_w, up_w, act, s1, s2, s3):
    place_activation(idx[0], idx[1], own, other, act, range(4))
    flush(0)
    partials(idx[3], (gate_w, up_w), act, (s1, s2, s3), flush)


def keep_kernel(flush, idx, act, gate_w, up_w, keep):
    kept(idx[3], (gate_w, up_w), act, keep)


def second_kernel(flush, idx, own, other, down, act, weight, keep, s1, s2, s3):
    for x in range(4):
        weight[:, x * 256 : (x + 1) * 256] = down[x]
    order = [lax.rem(idx[2] + 4 - k, 4) for k in range(4)]
    flush(1)
    place_activation(idx[0], idx[1], own, other, act, order)
    flush(0)
    partials(idx[3], (weight,), act, (s1, s2, s3), lambda k: None)
    kept(idx[3], (weight,), act, keep)


def place_hidden(idx, n, pieces, whole):
    y, lo = idx[3], idx[4]
    for k, piece in enumerate(pieces):
        start = lax.rem(y + 4 - k, 4) * 256
        for j, half in ((0, lo), (1, 1 - lo)):
            for i in range(n):
                whole[i, :, rows_of(start + half * 128, 128)] = piece[j, i]


def place_columns(idx, core, weights, columns):
    for i, w in enumerate(weights):
        for k, mask in enumerate(SCATTERED):
            block = (idx[0] ^ mask) * 2 + core
            columns[i, :, k * 128 : (k + 1) * 128] = w[:, rows_of(block * 128, 128)]


def back_product(n, whole, columns, out):
    for t in range(4):
        rows = slice(t * 256, (t + 1) * 256)
        total = dot_tn(whole[0, :, rows], columns[0])
        for i in range(1, n):
            total = total + dot_tn(whole[i, :, rows], columns[i])
        out[rows, :] = total


def back_kernel(flush, idx, p0, p1, p2, p3, w, whole, own, other, columns):
    place_hidden(idx, 1, (p0, p1, p2, p3), whole)
    flush(0)
    for core, out in ((1 - idx[1], other), (idx[1], own)):
        place_columns(idx, core, (w,), columns)
        back_product(1, whole, columns, out)


def other_kernel(flush, idx, p0, p1, p2, p3, w0, w1, whole, other, mine, theirs):
    place_hidden(idx, 2, (p0, p1, p2, p3), whole)
    flush(0)
    place_columns(idx, 1 - idx[1], (w0, w1), theirs)
    back_product(2, whole, theirs, other)
    place_columns(idx, idx[1], (w0, w1), mine)


def own_kernel(flush, idx, whole, columns, own):
    back_product(2, whole, columns, own)


def product_kernel(flush, idx, hid, grad, out):
    for x in range(4):
        part = jnp.dot(hid[0], grad[:, x * 256 : (x + 1) * 256], preferred_element_type=F32)
        out[x] = part.astype(BF16)


def exchange_x(blocks):
    return lax.all_to_all(blocks, "gy", split_axis=0, concat_axis=0, tiled=True)


def together(values):
    return list(lax.optimization_barrier(tuple(values)))


def after(value, *others):
    return lax.optimization_barrier((value, others))[0]


def spread_x(block):
    return [block] + together([send(block, "gy", shift_x(k)) for k in (1, 2, 3)])


def send_y(parts):
    return together([send(part, "gz", shift_y(k)) for k, part in zip((1, 2, 3), parts)])


def sum_rows(keep, received, lo):
    total = keep
    for part in received:
        total = total + part.astype(F32)
    low, high = total[..., :128], total[..., 128:]
    mine = jnp.where(lo == 0, low, high)
    theirs = jnp.where(lo == 0, high, low)
    return mine + send(theirs, "gz", SWAP_LO)


def pair_rows(block):
    return jnp.stack([block, send(block, "gz", SWAP_LO)])


def spread_y(pair):
    return [pair] + together([send(pair, "gz", shift_y(k)) for k in (1, 2, 3)])


def sum_core(own, swapped):
    total = own + swapped
    return total[:256], [total[k * 256 : (k + 1) * 256].astype(BF16) for k in (1, 2, 3)]


def send_x(parts):
    return together([send(part, "gy", shift_x(-k)) for k, part in zip((1, 2, 3), parts)])


def sum_x(rows, received):
    for part in received:
        rows = rows + part.astype(F32)
    return rows


def gather_hi(block):
    pair = jnp.stack([block, send(block, "gx", SWAP_HI_NEAR)])
    return jnp.concatenate([pair, send(pair, "gx", SWAP_HI_FAR)])


def send_near(rows):
    return send(rows[:, 256:].astype(BF16), "gx", SWAP_HI_NEAR)


def sum_columns_hi(rows, near):
    rows = rows[:, :256] + near.astype(F32)
    far = send(rows[:, 128:].astype(BF16), "gx", SWAP_HI_FAR)
    return (rows[:, :128] + far.astype(F32)).astype(BF16)


def local(tokens, gate_weight, up_weight, down_weight, out_grad):
    gx, gy, gz = lax.axis_index("gx"), lax.axis_index("gy"), lax.axis_index("gz")
    lo = gz // 4
    idx = jnp.stack([gx // 2, gx % 2, gy, gz % 4, lo]).astype(jnp.int32)
    gate_w, up_w = gate_weight.T, up_weight.T

    down = exchange_x(down_weight.reshape(4, 448, 256))
    tok_hi = gather_hi(tokens)
    tok_blocks = spread_x(tok_hi)
    grad_hi = gather_hi(after(out_grad, tok_hi))
    tok_own = jnp.stack(after(tok_blocks, down, grad_hi))
    tok_other = send(tok_own, "gx", SWAP_CORE)
    grad_own = exchange_x(jnp.broadcast_to(after(grad_hi, tok_own), (4, 4, 256, 128)))
    msg = [shape((2, 448, 256), BF16)] * 3
    tok, *gu_parts = call(
        first_kernel,
        [shape((1024, 1024), BF16)] + msg,
        (idx, tok_own, tok_other, gate_w, up_w),
        (2, 3),
        (0, 1, 2, 3),
    )
    gu_received = send_y(gu_parts)
    (gu_keep,) = call(
        keep_kernel,
        [shape((2, 448, 256), F32)],
        (idx, tok, gate_w, up_w),
        (0, 1, 2),
    )
    gu_received = after(gu_received, gu_keep)
    grad_other = send(after(grad_own, gu_received), "gx", SWAP_CORE)
    msg = [shape((1, 448, 256), BF16)] * 3
    grad, down_w, dh_keep, *dh_parts = call(
        second_kernel,
        [shape((1024, 1024), BF16), shape((448, 1024), BF16), shape((1, 448, 256), F32)] + msg,
        (idx, grad_own, grad_other, down),
        (2,),
        (0, 1),
    )
    gate_up = sum_rows(gu_keep, gu_received, lo)
    dh = sum_rows(dh_keep, send_y(dh_parts), lo)[0]
    gate, up = gate_up[0], gate_up[1]
    sig = jax.nn.sigmoid(gate)
    act = gate * sig
    hidden = (act * up).astype(BF16)
    gate_delta = (dh * up * sig * (1.0 + gate * (1.0 - sig))).astype(BF16)
    up_delta = (dh * act).astype(BF16)

    hid_pair = pair_rows(hidden[None])
    hid_pieces = spread_y(hid_pair)
    delta_pair = pair_rows(after(jnp.stack([gate_delta, up_delta]), hid_pair))
    delta_pieces = spread_y(delta_pair)
    hid_pieces = after(hid_pieces, delta_pair)
    hid, mixed_own, mixed_other = call(
        back_kernel,
        [shape((1, 448, 1024), BF16), shape((1024, 512), F32), shape((1024, 512), F32)],
        (idx, *hid_pieces, down_w),
        (4,),
        (0,),
        [pltpu.VMEM((1, 448, 512), BF16)],
    )
    mixed_rows, mixed_parts = sum_core(mixed_own, send(mixed_other, "gx", SWAP_CORE))
    mixed_received = send_x(mixed_parts)
    mixed_rows = sum_x(mixed_rows, mixed_received)
    delta_pieces = after(delta_pieces, mixed_received)
    delta, dx_other, dx_columns = call(
        other_kernel,
        [shape((2, 448, 1024), BF16), shape((1024, 512), F32), shape((2, 448, 512), BF16)],
        (idx, *delta_pieces, gate_w, up_w),
        (4, 5),
        (0,),
        [pltpu.VMEM((2, 448, 512), BF16)],
    )
    dx_swapped = send(dx_other, "gx", SWAP_CORE)
    (dx_own,) = call(own_kernel, [shape((1024, 512), F32)], (idx, delta, dx_columns), (0,))
    dx_rows, dx_parts = sum_core(dx_own, dx_swapped)
    (product,) = call(
        product_kernel,
        [shape((4, 448, 256), BF16)],
        (idx, after(hid, dx_parts), grad),
        (0, 1),
    )
    down_grad = exchange_x(product).reshape(1792, 256)
    delta = after(delta, dx_parts)
    mixed_near = send_near(after(mixed_rows, dx_parts))
    dx_received = after(send_x(dx_parts), mixed_near, product)
    mixed = sum_columns_hi(mixed_rows, mixed_near)
    down_grad = after(down_grad, dx_received)
    dx_rows = sum_x(dx_rows, dx_received)
    tokens_grad = sum_columns_hi(dx_rows, send_near(dx_rows))

    gate_grad = jnp.dot(delta[0], tok, preferred_element_type=F32).astype(BF16).T
    up_grad = jnp.dot(delta[1], tok, preferred_element_type=F32).astype(BF16).T
    return mixed, tokens_grad, gate_grad, up_grad, down_grad


def solution(mesh):
    in_specs = (
        P("gy", ("gz", "gx")),
        P("gz", ("gx", "gy")),
        P("gz", ("gx", "gy")),
        P("gx", ("gz", "gy")),
        P("gy", ("gz", "gx")),
    )
    out_specs = (
        P("gy", ("gz", "gx")),
        P("gy", ("gz", "gx")),
        P("gz", ("gx", "gy")),
        P("gz", ("gx", "gy")),
        P("gx", ("gz", "gy")),
    )
    return jax.shard_map(local, mesh=mesh, in_specs=in_specs, out_specs=out_specs, check_vma=False)
```

```python
import jax
import jax.numpy as jnp
from jax import lax
from jax.experimental import pallas as pl
from jax.experimental.pallas import tpu as pltpu
from jax.sharding import PartitionSpec as P

F32 = jnp.float32
BF16 = jnp.bfloat16
VMEM_LIMIT = 24 * 1024 * 1024


def shift_x(k):
    return [(g, (g + k) % 4) for g in range(4)]


def shift_y(k):
    return [(z * 4 + y, z * 4 + (y + k) % 4) for z in range(2) for y in range(4)]


SWAP_CORE = [(i, i ^ 1) for i in range(8)]
SWAP_LO = [(i, i ^ 4) for i in range(8)]
SWAP_HI_NEAR = [(i, i ^ 2) for i in range(8)]
SWAP_HI_FAR = [(i, i ^ 6) for i in range(8)]


def send(value, axis, moves):
    return lax.ppermute(value, axis, moves)


def staged(kernel, n_in, outs, far, n_scratch):
    n_out = len(outs)

    def run(idx, *refs):
        inputs, results = refs[:n_in], refs[n_in : n_in + n_out]
        scratch = refs[n_in + n_out : n_in + n_out + n_scratch]
        held = refs[n_in + n_out + n_scratch : -1]
        held, near, sems = held[:n_in], held[n_in:], refs[-1]
        copies = [
            pltpu.make_async_copy(src, dst, sems.at[i])
            for i, (src, dst) in enumerate(zip(inputs, held))
        ]
        for copy in copies:
            copy.start()
        for copy in copies:
            copy.wait()
        local_results = list(results)
        for i, ref in zip(far, near):
            local_results[i] = ref
        leaving = {
            i: pltpu.make_async_copy(ref, results[i], sems.at[n_in + n])
            for n, (i, ref) in enumerate(zip(far, near))
        }
        kernel(lambda i: leaving[i].start(), idx, *held, *local_results, *scratch)
        for i in far:
            leaving[i].wait()

    return run


def call(kernel, outs, args, far_in=(), far=(), scratch=()):
    n = len(args) - 1
    return pl.pallas_call(
        staged(kernel, n, outs, far, len(scratch)),
        out_shape=[
            pltpu.HBM(o.shape, o.dtype) if i in far else o for i, o in enumerate(outs)
        ],
        in_specs=[pl.BlockSpec(memory_space=pltpu.SMEM)]
        + [pl.BlockSpec(memory_space=pltpu.HBM if i in far_in else pl.ANY) for i in range(n)],
        out_specs=[
            pl.BlockSpec(memory_space=pltpu.HBM if i in far else pltpu.VMEM)
            for i in range(len(outs))
        ],
        scratch_shapes=list(scratch)
        + [pltpu.VMEM(a.shape, a.dtype) for a in args[1:]]
        + [pltpu.VMEM(outs[i].shape, outs[i].dtype) for i in far]
        + [pltpu.SemaphoreType.DMA((n + len(far),))],
        compiler_params=pltpu.CompilerParams(vmem_limit_bytes=VMEM_LIMIT),
        cost_estimate=pl.CostEstimate(flops=1, bytes_accessed=1, transcendentals=0),
    )(
        args[0],
        *[
            pltpu.with_memory_space_constraint(a, pltpu.HBM) if i in far_in else a
            for i, a in enumerate(args[1:])
        ],
    )


def shape(dims, dtype):
    return jax.ShapeDtypeStruct(dims, dtype)


def dot_nt(left, right):
    return lax.dot_general(left, right, (((1,), (1,)), ((), ())), preferred_element_type=F32)


def dot_tn(left, right):
    return lax.dot_general(left, right, (((0,), (0,)), ((), ())), preferred_element_type=F32)


def rows_of(start, size):
    return pl.ds(pl.multiple_of(start, size), size)


GATHERED = (0, 1, 3, 2)
SCATTERED = (0, 3, 1, 2)


def place_activation(hi, core, own_ref, other_ref, act_ref, order):
    for slot, mask in enumerate(GATHERED):
        block = (hi ^ mask) * 2
        for x in range(4):
            rows = slice(x * 256, (x + 1) * 256)
            act_ref[rows, rows_of((block + core) * 128, 128)] = own_ref[order[x], slot]
            act_ref[rows, rows_of((block + 1 - core) * 128, 128)] = other_ref[order[x], slot]


def partials(y, weights, act_ref, sends, sent):
    for k in (2, 1, 3):
        act = act_ref[rows_of(lax.rem(y + k, 4) * 256, 256), :]
        for i, w_ref in enumerate(weights):
            sends[k - 1][i] = dot_nt(w_ref[...], act).astype(BF16)
        sent(k)


def kept(y, weights, act_ref, keep_ref):
    act = act_ref[rows_of(y * 256, 256), :]
    for i, w_ref in enumerate(weights):
        keep_ref[i] = dot_nt(w_ref[...], act)


def first_kernel(flush, idx, own, other, gate_w, up_w, act, s1, s2, s3):
    place_activation(idx[0], idx[1], own, other, act, range(4))
    flush(0)
    partials(idx[3], (gate_w, up_w), act, (s1, s2, s3), flush)


def keep_kernel(flush, idx, act, gate_w, up_w, keep):
    kept(idx[3], (gate_w, up_w), act, keep)


def second_kernel(flush, idx, own, other, down, act, weight, keep, s1, s2, s3):
    for x in range(4):
        weight[:, x * 256 : (x + 1) * 256] = down[x]
    order = [lax.rem(idx[2] + 4 - k, 4) for k in range(4)]
    flush(1)
    place_activation(idx[0], idx[1], own, other, act, order)
    flush(0)
    partials(idx[3], (weight,), act, (s1, s2, s3), lambda k: None)
    kept(idx[3], (weight,), act, keep)


def place_hidden(idx, n, pieces, whole):
    y, lo = idx[3], idx[4]
    for k, piece in enumerate(pieces):
        start = lax.rem(y + 4 - k, 4) * 256
        for j, half in ((0, lo), (1, 1 - lo)):
            for i in range(n):
                whole[i, :, rows_of(start + half * 128, 128)] = piece[j, i]


def place_columns(idx, core, weights, columns):
    for i, w in enumerate(weights):
        for k, mask in enumerate(SCATTERED):
            block = (idx[0] ^ mask) * 2 + core
            columns[i, :, k * 128 : (k + 1) * 128] = w[:, rows_of(block * 128, 128)]


def back_product(n, whole, columns, out):
    for t in range(4):
        rows = slice(t * 256, (t + 1) * 256)
        total = dot_tn(whole[0, :, rows], columns[0])
        for i in range(1, n):
            total = total + dot_tn(whole[i, :, rows], columns[i])
        out[rows, :] = total


def back_kernel(flush, idx, p0, p1, p2, p3, w, whole, own, other, columns):
    place_hidden(idx, 1, (p0, p1, p2, p3), whole)
    flush(0)
    for core, out in ((1 - idx[1], other), (idx[1], own)):
        place_columns(idx, core, (w,), columns)
        back_product(1, whole, columns, out)


def other_kernel(flush, idx, p0, p1, p2, p3, w0, w1, whole, other, mine, theirs):
    place_hidden(idx, 2, (p0, p1, p2, p3), whole)
    flush(0)
    place_columns(idx, 1 - idx[1], (w0, w1), theirs)
    back_product(2, whole, theirs, other)
    place_columns(idx, idx[1], (w0, w1), mine)


def own_kernel(flush, idx, whole, columns, own):
    back_product(2, whole, columns, own)


def product_kernel(flush, idx, hid, grad, out):
    for x in range(4):
        part = jnp.dot(hid[0], grad[:, x * 256 : (x + 1) * 256], preferred_element_type=F32)
        out[x] = part.astype(BF16)


def exchange_x(blocks):
    return lax.all_to_all(blocks, "gy", split_axis=0, concat_axis=0, tiled=True)


def together(values):
    return list(lax.optimization_barrier(tuple(values)))


def after(value, *others):
    return lax.optimization_barrier((value, others))[0]


def spread_x(block):
    return [block] + together([send(block, "gy", shift_x(k)) for k in (1, 2, 3)])


def send_y(parts):
    return together([send(part, "gz", shift_y(k)) for k, part in zip((1, 2, 3), parts)])


def sum_rows(keep, received, lo):
    total = keep
    for part in received:
        total = total + part.astype(F32)
    low, high = total[..., :128], total[..., 128:]
    mine = jnp.where(lo == 0, low, high)
    theirs = jnp.where(lo == 0, high, low)
    return mine + send(theirs, "gz", SWAP_LO)


def pair_rows(block):
    return jnp.stack([block, send(block, "gz", SWAP_LO)])


def spread_y(pair):
    return [pair] + together([send(pair, "gz", shift_y(k)) for k in (1, 2, 3)])


def sum_core(own, swapped):
    total = own + swapped
    return total[:256], [total[k * 256 : (k + 1) * 256].astype(BF16) for k in (1, 2, 3)]


def send_x(parts):
    return together([send(part, "gy", shift_x(-k)) for k, part in zip((1, 2, 3), parts)])


def sum_x(rows, received):
    for part in received:
        rows = rows + part.astype(F32)
    return rows


def pair_hi(block):
    return jnp.stack([block, send(block, "gx", SWAP_HI_NEAR)])


def gather_hi(pair):
    return jnp.concatenate([pair, send(pair, "gx", SWAP_HI_FAR)])


def send_near(rows):
    return send(rows[:, 256:].astype(BF16), "gx", SWAP_HI_NEAR)


def sum_columns_hi(rows, near):
    rows = rows[:, :256] + near.astype(F32)
    far = send(rows[:, 128:].astype(BF16), "gx", SWAP_HI_FAR)
    return (rows[:, :128] + far.astype(F32)).astype(BF16)


def local(tokens, gate_weight, up_weight, down_weight, out_grad):
    gx, gy, gz = lax.axis_index("gx"), lax.axis_index("gy"), lax.axis_index("gz")
    lo = gz // 4
    idx = jnp.stack([gx // 2, gx % 2, gy, gz % 4, lo]).astype(jnp.int32)
    gate_w, up_w = gate_weight.T, up_weight.T

    tok_pair = pair_hi(tokens)
    down = exchange_x(after(down_weight, tok_pair).reshape(4, 448, 256))
    tok_hi = gather_hi(tok_pair)
    tok_blocks = spread_x(tok_hi)
    grad_hi = gather_hi(pair_hi(after(out_grad, tok_pair)))
    tok_own = jnp.stack(after(tok_blocks, down, grad_hi))
    tok_other = send(tok_own, "gx", SWAP_CORE)
    grad_own = exchange_x(after(jnp.broadcast_to(grad_hi, (4, 4, 256, 128)), tok_own))
    msg = [shape((2, 448, 256), BF16)] * 3
    tok, *gu_parts = call(
        first_kernel,
        [shape((1024, 1024), BF16)] + msg,
        (idx, tok_own, tok_other, gate_w, up_w),
        (2, 3),
        (0, 1, 2, 3),
    )
    gu_received = send_y(gu_parts)
    (gu_keep,) = call(
        keep_kernel,
        [shape((2, 448, 256), F32)],
        (idx, tok, gate_w, up_w),
        (0, 1, 2),
    )
    gu_received = after(gu_received, gu_keep)
    grad_other = send(after(grad_own, gu_received), "gx", SWAP_CORE)
    msg = [shape((1, 448, 256), BF16)] * 3
    grad, down_w, dh_keep, *dh_parts = call(
        second_kernel,
        [shape((1024, 1024), BF16), shape((448, 1024), BF16), shape((1, 448, 256), F32)] + msg,
        (idx, grad_own, grad_other, down),
        (2,),
        (0, 1),
    )
    gate_up = sum_rows(gu_keep, gu_received, lo)
    dh = sum_rows(dh_keep, send_y(dh_parts), lo)[0]
    gate, up = gate_up[0], gate_up[1]
    sig = jax.nn.sigmoid(gate)
    act = gate * sig
    hidden = (act * up).astype(BF16)
    gate_delta = (dh * up * sig * (1.0 + gate * (1.0 - sig))).astype(BF16)
    up_delta = (dh * act).astype(BF16)

    hid_pair = pair_rows(hidden[None])
    hid_pieces = spread_y(hid_pair)
    delta_pair = pair_rows(after(jnp.stack([gate_delta, up_delta]), hid_pair))
    delta_pieces = spread_y(delta_pair)
    hid_pieces = after(hid_pieces, delta_pair)
    hid, mixed_own, mixed_other = call(
        back_kernel,
        [shape((1, 448, 1024), BF16), shape((1024, 512), F32), shape((1024, 512), F32)],
        (idx, *hid_pieces, down_w),
        (4,),
        (0,),
        [pltpu.VMEM((1, 448, 512), BF16)],
    )
    mixed_rows, mixed_parts = sum_core(mixed_own, send(mixed_other, "gx", SWAP_CORE))
    mixed_received = send_x(mixed_parts)
    mixed_rows = sum_x(mixed_rows, mixed_received)
    (product,) = call(
        product_kernel,
        [shape((4, 448, 256), BF16)],
        (idx, hid, grad),
        (0, 1),
    )
    delta_pieces = after(delta_pieces, mixed_received, product)
    delta, dx_other, dx_columns = call(
        other_kernel,
        [shape((2, 448, 1024), BF16), shape((1024, 512), F32), shape((2, 448, 512), BF16)],
        (idx, *delta_pieces, gate_w, up_w),
        (4, 5),
        (0,),
        [pltpu.VMEM((2, 448, 512), BF16)],
    )
    dx_swapped = send(dx_other, "gx", SWAP_CORE)
    (dx_own,) = call(own_kernel, [shape((1024, 512), F32)], (idx, delta, dx_columns), (0,))
    dx_rows, dx_parts = sum_core(dx_own, dx_swapped)
    down_grad = exchange_x(after(product, dx_parts)).reshape(1792, 256)
    mixed_near = send_near(after(mixed_rows, dx_parts))
    dx_received = after(send_x(dx_parts), mixed_near)
    delta = after(delta, dx_parts)
    mixed = sum_columns_hi(mixed_rows, mixed_near)
    down_grad = after(down_grad, dx_received)
    dx_rows = sum_x(dx_rows, dx_received)
    tokens_grad = sum_columns_hi(dx_rows, send_near(dx_rows))

    gate_grad = jnp.dot(delta[0], tok, preferred_element_type=F32).astype(BF16).T
    up_grad = jnp.dot(delta[1], tok, preferred_element_type=F32).astype(BF16).T
    return mixed, tokens_grad, gate_grad, up_grad, down_grad


def solution(mesh):
    in_specs = (
        P("gy", ("gz", "gx")),
        P("gz", ("gx", "gy")),
        P("gz", ("gx", "gy")),
        P("gx", ("gz", "gy")),
        P("gy", ("gz", "gx")),
    )
    out_specs = (
        P("gy", ("gz", "gx")),
        P("gy", ("gz", "gx")),
        P("gz", ("gx", "gy")),
        P("gz", ("gx", "gy")),
        P("gx", ("gz", "gy")),
    )
    return jax.shard_map(local, mesh=mesh, in_specs=in_specs, out_specs=out_specs, check_vma=False)
```

```python
import jax
import jax.numpy as jnp
from jax import lax
from jax.experimental import pallas as pl
from jax.experimental.pallas import tpu as pltpu
from jax.sharding import PartitionSpec as P

F32 = jnp.float32
BF16 = jnp.bfloat16
VMEM_LIMIT = 24 * 1024 * 1024


def shift_x(k):
    return [(g, (g + k) % 4) for g in range(4)]


def shift_y(k):
    return [(z * 4 + y, z * 4 + (y + k) % 4) for z in range(2) for y in range(4)]


SWAP_CORE = [(i, i ^ 1) for i in range(8)]
SWAP_LO = [(i, i ^ 4) for i in range(8)]
SWAP_HI_NEAR = [(i, i ^ 2) for i in range(8)]
SWAP_HI_FAR = [(i, i ^ 6) for i in range(8)]


def send(value, axis, moves):
    return lax.ppermute(value, axis, moves)


def staged(kernel, n_in, outs, far, n_scratch):
    n_out = len(outs)

    def run(idx, *refs):
        inputs, results = refs[:n_in], refs[n_in : n_in + n_out]
        scratch = refs[n_in + n_out : n_in + n_out + n_scratch]
        held = refs[n_in + n_out + n_scratch : -1]
        held, near, sems = held[:n_in], held[n_in:], refs[-1]
        copies = [
            pltpu.make_async_copy(src, dst, sems.at[i])
            for i, (src, dst) in enumerate(zip(inputs, held))
        ]
        for copy in copies:
            copy.start()
        for copy in copies:
            copy.wait()
        local_results = list(results)
        for i, ref in zip(far, near):
            local_results[i] = ref
        leaving = {
            i: pltpu.make_async_copy(ref, results[i], sems.at[n_in + n])
            for n, (i, ref) in enumerate(zip(far, near))
        }
        kernel(lambda i: leaving[i].start(), idx, *held, *local_results, *scratch)
        for i in far:
            leaving[i].wait()

    return run


def call(kernel, outs, args, far_in=(), far=(), scratch=()):
    n = len(args) - 1
    return pl.pallas_call(
        staged(kernel, n, outs, far, len(scratch)),
        out_shape=[
            pltpu.HBM(o.shape, o.dtype) if i in far else o for i, o in enumerate(outs)
        ],
        in_specs=[pl.BlockSpec(memory_space=pltpu.SMEM)]
        + [pl.BlockSpec(memory_space=pltpu.HBM if i in far_in else pl.ANY) for i in range(n)],
        out_specs=[
            pl.BlockSpec(memory_space=pltpu.HBM if i in far else pltpu.VMEM)
            for i in range(len(outs))
        ],
        scratch_shapes=list(scratch)
        + [pltpu.VMEM(a.shape, a.dtype) for a in args[1:]]
        + [pltpu.VMEM(outs[i].shape, outs[i].dtype) for i in far]
        + [pltpu.SemaphoreType.DMA((n + len(far),))],
        compiler_params=pltpu.CompilerParams(vmem_limit_bytes=VMEM_LIMIT),
        cost_estimate=pl.CostEstimate(flops=1, bytes_accessed=1, transcendentals=0),
    )(
        args[0],
        *[
            pltpu.with_memory_space_constraint(a, pltpu.HBM) if i in far_in else a
            for i, a in enumerate(args[1:])
        ],
    )


def shape(dims, dtype):
    return jax.ShapeDtypeStruct(dims, dtype)


def dot_nt(left, right):
    return lax.dot_general(left, right, (((1,), (1,)), ((), ())), preferred_element_type=F32)


def dot_tn(left, right):
    return lax.dot_general(left, right, (((0,), (0,)), ((), ())), preferred_element_type=F32)


def rows_of(start, size):
    return pl.ds(pl.multiple_of(start, size), size)


GATHERED = (0, 1, 3, 2)
SCATTERED = (0, 3, 1, 2)


def place_activation(hi, core, own_ref, other_ref, act_ref, order):
    for slot, mask in enumerate(GATHERED):
        block = (hi ^ mask) * 2
        for x in range(4):
            rows = slice(x * 256, (x + 1) * 256)
            act_ref[rows, rows_of((block + core) * 128, 128)] = own_ref[order[x], slot]
            act_ref[rows, rows_of((block + 1 - core) * 128, 128)] = other_ref[order[x], slot]


def partials(y, weights, act_ref, sends, sent):
    for k in (2, 1, 3):
        act = act_ref[rows_of(lax.rem(y + k, 4) * 256, 256), :]
        for i, w_ref in enumerate(weights):
            sends[k - 1][i] = dot_nt(w_ref[...], act).astype(BF16)
        sent(k)


def kept(y, weights, act_ref, keep_ref):
    act = act_ref[rows_of(y * 256, 256), :]
    for i, w_ref in enumerate(weights):
        keep_ref[i] = dot_nt(w_ref[...], act)


def first_kernel(flush, idx, own, other, gate_w, up_w, act, s1, s2, s3):
    place_activation(idx[0], idx[1], own, other, act, range(4))
    flush(0)
    partials(idx[3], (gate_w, up_w), act, (s1, s2, s3), flush)


def keep_kernel(flush, idx, act, gate_w, up_w, keep):
    kept(idx[3], (gate_w, up_w), act, keep)


def second_kernel(flush, idx, own, other, down, act, weight, keep, s1, s2, s3):
    for x in range(4):
        weight[:, x * 256 : (x + 1) * 256] = down[x]
    order = [lax.rem(idx[2] + 4 - k, 4) for k in range(4)]
    flush(1)
    place_activation(idx[0], idx[1], own, other, act, order)
    flush(0)
    partials(idx[3], (weight,), act, (s1, s2, s3), lambda k: None)
    kept(idx[3], (weight,), act, keep)


def place_hidden(idx, n, pieces, whole):
    y, lo = idx[3], idx[4]
    for k, piece in enumerate(pieces):
        start = lax.rem(y + 4 - k, 4) * 256
        for j, half in ((0, lo), (1, 1 - lo)):
            for i in range(n):
                whole[i, :, rows_of(start + half * 128, 128)] = piece[j, i]


def place_columns(idx, core, weights, columns):
    for i, w in enumerate(weights):
        for k, mask in enumerate(SCATTERED):
            block = (idx[0] ^ mask) * 2 + core
            columns[i, :, k * 128 : (k + 1) * 128] = w[:, rows_of(block * 128, 128)]


def back_product(n, whole, columns, out):
    for t in range(4):
        rows = slice(t * 256, (t + 1) * 256)
        total = dot_tn(whole[0, :, rows], columns[0])
        for i in range(1, n):
            total = total + dot_tn(whole[i, :, rows], columns[i])
        out[rows, :] = total


def other_kernel(flush, idx, p0, p1, p2, p3, *refs):
    weights, (whole, other, mine, theirs) = refs[:-4], refs[-4:]
    n = len(weights)
    place_hidden(idx, n, (p0, p1, p2, p3), whole)
    flush(0)
    place_columns(idx, 1 - idx[1], weights, theirs)
    back_product(n, whole, theirs, other)
    place_columns(idx, idx[1], weights, mine)


def own_kernel(flush, idx, whole, columns, own):
    back_product(whole.shape[0], whole, columns, own)


def product_kernel(flush, idx, hid, grad, out):
    for x in range(4):
        part = jnp.dot(hid[0], grad[:, x * 256 : (x + 1) * 256], preferred_element_type=F32)
        out[x] = part.astype(BF16)


def exchange_x(blocks):
    return lax.all_to_all(blocks, "gy", split_axis=0, concat_axis=0, tiled=True)


def together(values):
    return list(lax.optimization_barrier(tuple(values)))


def after(value, *others):
    return lax.optimization_barrier((value, others))[0]


def spread_x(block):
    return [block] + together([send(block, "gy", shift_x(k)) for k in (1, 2, 3)])


def send_y(parts):
    return together([send(part, "gz", shift_y(k)) for k, part in zip((1, 2, 3), parts)])


def sum_rows(keep, received, lo):
    total = keep
    for part in received:
        total = total + part.astype(F32)
    low, high = total[..., :128], total[..., 128:]
    mine = jnp.where(lo == 0, low, high)
    theirs = jnp.where(lo == 0, high, low)
    return mine + send(theirs, "gz", SWAP_LO)


def pair_rows(block):
    return jnp.stack([block, send(block, "gz", SWAP_LO)])


def spread_y(pair):
    return [pair] + together([send(pair, "gz", shift_y(k)) for k in (1, 2, 3)])


def sum_core(own, swapped):
    total = own + swapped
    return total[:256], [total[k * 256 : (k + 1) * 256].astype(BF16) for k in (1, 2, 3)]


def send_x(parts):
    return together([send(part, "gy", shift_x(-k)) for k, part in zip((1, 2, 3), parts)])


def sum_x(rows, received):
    for part in received:
        rows = rows + part.astype(F32)
    return rows


def pair_hi(block):
    return jnp.stack([block, send(block, "gx", SWAP_HI_NEAR)])


def gather_hi(pair):
    return jnp.concatenate([pair, send(pair, "gx", SWAP_HI_FAR)])


def send_near(rows):
    return send(rows[:, 256:].astype(BF16), "gx", SWAP_HI_NEAR)


def sum_columns_hi(rows, near):
    rows = rows[:, :256] + near.astype(F32)
    far = send(rows[:, 128:].astype(BF16), "gx", SWAP_HI_FAR)
    return (rows[:, :128] + far.astype(F32)).astype(BF16)


def local(tokens, gate_weight, up_weight, down_weight, out_grad):
    gx, gy, gz = lax.axis_index("gx"), lax.axis_index("gy"), lax.axis_index("gz")
    lo = gz // 4
    idx = jnp.stack([gx // 2, gx % 2, gy, gz % 4, lo]).astype(jnp.int32)
    gate_w, up_w = gate_weight.T, up_weight.T

    tok_pair = pair_hi(tokens)
    down = exchange_x(after(down_weight, tok_pair).reshape(4, 448, 256))
    tok_hi = gather_hi(tok_pair)
    tok_blocks = spread_x(tok_hi)
    grad_hi = gather_hi(pair_hi(after(out_grad, tok_pair)))
    tok_own = jnp.stack(after(tok_blocks, down, grad_hi))
    tok_other = send(tok_own, "gx", SWAP_CORE)
    grad_own = exchange_x(after(jnp.broadcast_to(grad_hi, (4, 4, 256, 128)), tok_own))
    msg = [shape((2, 448, 256), BF16)] * 3
    tok, *gu_parts = call(
        first_kernel,
        [shape((1024, 1024), BF16)] + msg,
        (idx, tok_own, tok_other, gate_w, up_w),
        (2, 3),
        (0, 1, 2, 3),
    )
    gu_received = send_y(gu_parts)
    (gu_keep,) = call(
        keep_kernel,
        [shape((2, 448, 256), F32)],
        (idx, tok, gate_w, up_w),
        (0, 1, 2),
    )
    gu_received = after(gu_received, gu_keep)
    grad_other = send(after(grad_own, gu_received), "gx", SWAP_CORE)
    msg = [shape((1, 448, 256), BF16)] * 3
    grad, down_w, dh_keep, *dh_parts = call(
        second_kernel,
        [shape((1024, 1024), BF16), shape((448, 1024), BF16), shape((1, 448, 256), F32)] + msg,
        (idx, grad_own, grad_other, down),
        (2,),
        (0, 1),
    )
    gate_up = sum_rows(gu_keep, gu_received, lo)
    dh = sum_rows(dh_keep, send_y(dh_parts), lo)[0]
    gate, up = gate_up[0], gate_up[1]
    sig = jax.nn.sigmoid(gate)
    act = gate * sig
    hidden = (act * up).astype(BF16)
    gate_delta = (dh * up * sig * (1.0 + gate * (1.0 - sig))).astype(BF16)
    up_delta = (dh * act).astype(BF16)

    hid_pair = pair_rows(hidden[None])
    hid_pieces = spread_y(hid_pair)
    delta_pair = pair_rows(after(jnp.stack([gate_delta, up_delta]), hid_pair))
    delta_pieces = spread_y(delta_pair)
    hid_pieces = after(hid_pieces, delta_pair)
    hid, mixed_other, mixed_columns = call(
        other_kernel,
        [shape((1, 448, 1024), BF16), shape((1024, 512), F32), shape((1, 448, 512), BF16)],
        (idx, *hid_pieces, down_w),
        (4,),
        (0,),
        [pltpu.VMEM((1, 448, 512), BF16)],
    )
    mixed_swapped = send(mixed_other, "gx", SWAP_CORE)
    (mixed_own,) = call(own_kernel, [shape((1024, 512), F32)], (idx, hid, mixed_columns), (0,))
    mixed_rows, mixed_parts = sum_core(mixed_own, mixed_swapped)
    mixed_received = send_x(mixed_parts)
    mixed_rows = sum_x(mixed_rows, mixed_received)
    (product,) = call(
        product_kernel,
        [shape((4, 448, 256), BF16)],
        (idx, hid, grad),
        (0, 1),
    )
    delta_pieces = after(delta_pieces, mixed_received, product)
    delta, dx_other, dx_columns = call(
        other_kernel,
        [shape((2, 448, 1024), BF16), shape((1024, 512), F32), shape((2, 448, 512), BF16)],
        (idx, *delta_pieces, gate_w, up_w),
        (4, 5),
        (0,),
        [pltpu.VMEM((2, 448, 512), BF16)],
    )
    dx_swapped = send(dx_other, "gx", SWAP_CORE)
    (dx_own,) = call(own_kernel, [shape((1024, 512), F32)], (idx, delta, dx_columns), (0,))
    dx_rows, dx_parts = sum_core(dx_own, dx_swapped)
    down_grad = exchange_x(after(product, dx_parts)).reshape(1792, 256)
    mixed_near = send_near(after(mixed_rows, dx_parts))
    dx_received = after(send_x(dx_parts), mixed_near)
    delta = after(delta, dx_parts)
    mixed = sum_columns_hi(mixed_rows, mixed_near)
    down_grad = after(down_grad, dx_received)
    dx_rows = sum_x(dx_rows, dx_received)
    tokens_grad = sum_columns_hi(dx_rows, send_near(dx_rows))

    gate_grad = jnp.dot(delta[0], tok, preferred_element_type=F32).astype(BF16).T
    up_grad = jnp.dot(delta[1], tok, preferred_element_type=F32).astype(BF16).T
    return mixed, tokens_grad, gate_grad, up_grad, down_grad


def solution(mesh):
    in_specs = (
        P("gy", ("gz", "gx")),
        P("gz", ("gx", "gy")),
        P("gz", ("gx", "gy")),
        P("gx", ("gz", "gy")),
        P("gy", ("gz", "gx")),
    )
    out_specs = (
        P("gy", ("gz", "gx")),
        P("gy", ("gz", "gx")),
        P("gz", ("gx", "gy")),
        P("gz", ("gx", "gy")),
        P("gx", ("gz", "gy")),
    )
    return jax.shard_map(local, mesh=mesh, in_specs=in_specs, out_specs=out_specs, check_vma=False)
```

```python
import jax
import jax.numpy as jnp
from jax import lax
from jax.experimental import pallas as pl
from jax.experimental.pallas import tpu as pltpu
from jax.sharding import PartitionSpec as P

F32 = jnp.float32
BF16 = jnp.bfloat16
VMEM_LIMIT = 24 * 1024 * 1024


def shift_x(k):
    return [(g, (g + k) % 4) for g in range(4)]


def shift_y(k):
    return [(z * 4 + y, z * 4 + (y + k) % 4) for z in range(2) for y in range(4)]


SWAP_CORE = [(i, i ^ 1) for i in range(8)]
SWAP_LO = [(i, i ^ 4) for i in range(8)]
SWAP_HI_NEAR = [(i, i ^ 2) for i in range(8)]
SWAP_HI_FAR = [(i, i ^ 6) for i in range(8)]


def send(value, axis, moves):
    return lax.ppermute(value, axis, moves)


def staged(kernel, n_in, outs, far, n_scratch):
    n_out = len(outs)

    def run(idx, *refs):
        inputs, results = refs[:n_in], refs[n_in : n_in + n_out]
        scratch = refs[n_in + n_out : n_in + n_out + n_scratch]
        held = refs[n_in + n_out + n_scratch : -1]
        held, near, sems = held[:n_in], held[n_in:], refs[-1]
        copies = [
            pltpu.make_async_copy(src, dst, sems.at[i])
            for i, (src, dst) in enumerate(zip(inputs, held))
        ]
        for copy in copies:
            copy.start()
        for copy in copies:
            copy.wait()
        local_results = list(results)
        for i, ref in zip(far, near):
            local_results[i] = ref
        leaving = {
            i: pltpu.make_async_copy(ref, results[i], sems.at[n_in + n])
            for n, (i, ref) in enumerate(zip(far, near))
        }
        kernel(lambda i: leaving[i].start(), idx, *held, *local_results, *scratch)
        for i in far:
            leaving[i].wait()

    return run


def call(kernel, outs, args, far_in=(), far=(), scratch=()):
    n = len(args) - 1
    return pl.pallas_call(
        staged(kernel, n, outs, far, len(scratch)),
        out_shape=[
            pltpu.HBM(o.shape, o.dtype) if i in far else o for i, o in enumerate(outs)
        ],
        in_specs=[pl.BlockSpec(memory_space=pltpu.SMEM)]
        + [pl.BlockSpec(memory_space=pltpu.HBM if i in far_in else pl.ANY) for i in range(n)],
        out_specs=[
            pl.BlockSpec(memory_space=pltpu.HBM if i in far else pltpu.VMEM)
            for i in range(len(outs))
        ],
        scratch_shapes=list(scratch)
        + [pltpu.VMEM(a.shape, a.dtype) for a in args[1:]]
        + [pltpu.VMEM(outs[i].shape, outs[i].dtype) for i in far]
        + [pltpu.SemaphoreType.DMA((n + len(far),))],
        compiler_params=pltpu.CompilerParams(vmem_limit_bytes=VMEM_LIMIT),
        cost_estimate=pl.CostEstimate(flops=1, bytes_accessed=1, transcendentals=0),
    )(
        args[0],
        *[
            pltpu.with_memory_space_constraint(a, pltpu.HBM) if i in far_in else a
            for i, a in enumerate(args[1:])
        ],
    )


def shape(dims, dtype):
    return jax.ShapeDtypeStruct(dims, dtype)


def dot_nt(left, right):
    return lax.dot_general(left, right, (((1,), (1,)), ((), ())), preferred_element_type=F32)


def dot_tn(left, right):
    return lax.dot_general(left, right, (((0,), (0,)), ((), ())), preferred_element_type=F32)


def rows_of(start, size):
    return pl.ds(pl.multiple_of(start, size), size)


GATHERED = (0, 1, 3, 2)
SCATTERED = (0, 3, 1, 2)


def place_activation(hi, core, own_ref, other_ref, act_ref, order):
    for slot, mask in enumerate(GATHERED):
        block = (hi ^ mask) * 2
        for x in range(4):
            rows = slice(x * 256, (x + 1) * 256)
            act_ref[rows, rows_of((block + core) * 128, 128)] = own_ref[order[x], slot]
            act_ref[rows, rows_of((block + 1 - core) * 128, 128)] = other_ref[order[x], slot]


def partials(y, weights, act_ref, sends, sent):
    for k in (2, 1, 3):
        act = act_ref[rows_of(lax.rem(y + k, 4) * 256, 256), :]
        for i, w_ref in enumerate(weights):
            sends[k - 1][i] = dot_nt(w_ref[...], act).astype(BF16)
        sent(k)


def kept(y, weights, act_ref, keep_ref):
    act = act_ref[rows_of(y * 256, 256), :]
    for i, w_ref in enumerate(weights):
        keep_ref[i] = dot_nt(w_ref[...], act)


def first_kernel(flush, idx, own, other, gate_w, up_w, act, s1, s2, s3):
    place_activation(idx[0], idx[1], own, other, act, range(4))
    flush(0)
    partials(idx[3], (gate_w, up_w), act, (s1, s2, s3), flush)


def keep_kernel(flush, idx, act, gate_w, up_w, keep):
    kept(idx[3], (gate_w, up_w), act, keep)


def second_kernel(flush, idx, own, other, down, act, weight, keep, s1, s2, s3):
    for x in range(4):
        weight[:, x * 256 : (x + 1) * 256] = down[x]
    order = [lax.rem(idx[2] + 4 - k, 4) for k in range(4)]
    flush(1)
    place_activation(idx[0], idx[1], own, other, act, order)
    flush(0)
    partials(idx[3], (weight,), act, (s1, s2, s3), lambda k: None)
    kept(idx[3], (weight,), act, keep)


def place_hidden(idx, n, pieces, whole):
    y, lo = idx[3], idx[4]
    for k, piece in enumerate(pieces):
        start = lax.rem(y + 4 - k, 4) * 256
        for j, half in ((0, lo), (1, 1 - lo)):
            for i in range(n):
                whole[i, :, rows_of(start + half * 128, 128)] = piece[j, i]


def place_columns(idx, core, weights, columns):
    for i, w in enumerate(weights):
        for k, mask in enumerate(SCATTERED):
            block = (idx[0] ^ mask) * 2 + core
            columns[i, :, k * 128 : (k + 1) * 128] = w[:, rows_of(block * 128, 128)]


def back_product(n, whole, columns, out):
    for t in range(4):
        rows = slice(t * 256, (t + 1) * 256)
        total = dot_tn(whole[0, :, rows], columns[0])
        for i in range(1, n):
            total = total + dot_tn(whole[i, :, rows], columns[i])
        out[rows, :] = total


def other_kernel(flush, idx, p0, p1, p2, p3, *refs):
    weights, (whole, other, mine, theirs) = refs[:-4], refs[-4:]
    n = len(weights)
    place_hidden(idx, n, (p0, p1, p2, p3), whole)
    flush(0)
    place_columns(idx, 1 - idx[1], weights, theirs)
    back_product(n, whole, theirs, other)
    place_columns(idx, idx[1], weights, mine)


def own_kernel(flush, idx, whole, columns, own):
    back_product(whole.shape[0], whole, columns, own)


def product_kernel(flush, idx, hid, grad, out):
    for x in range(4):
        part = jnp.dot(hid[0], grad[:, x * 256 : (x + 1) * 256], preferred_element_type=F32)
        out[x] = part.astype(BF16)


def exchange_x(blocks):
    return lax.all_to_all(blocks, "gy", split_axis=0, concat_axis=0, tiled=True)


def together(values):
    return list(lax.optimization_barrier(tuple(values)))


def after(value, *others):
    return lax.optimization_barrier((value, others))[0]


def spread_x(block):
    return [block] + together([send(block, "gy", shift_x(k)) for k in (1, 2, 3)])


def send_y(parts):
    return together([send(part, "gz", shift_y(k)) for k, part in zip((1, 2, 3), parts)])


def sum_rows(keep, received, lo):
    total = keep
    for part in received:
        total = total + part.astype(F32)
    low, high = total[..., :128], total[..., 128:]
    mine = jnp.where(lo == 0, low, high)
    theirs = jnp.where(lo == 0, high, low)
    return mine + send(theirs, "gz", SWAP_LO)


def pair_rows(block):
    return jnp.stack([block, send(block, "gz", SWAP_LO)])


def spread_y(pair):
    return [pair] + together([send(pair, "gz", shift_y(k)) for k in (1, 2, 3)])


def sum_core(own, swapped):
    total = own + swapped
    return total[:256], [total[k * 256 : (k + 1) * 256].astype(BF16) for k in (1, 2, 3)]


def send_x(parts):
    return together([send(part, "gy", shift_x(-k)) for k, part in zip((1, 2, 3), parts)])


def sum_x(rows, received):
    for part in received:
        rows = rows + part.astype(F32)
    return rows


def pair_hi(block):
    return jnp.stack([block, send(block, "gx", SWAP_HI_NEAR)])


def gather_hi(pair):
    return jnp.concatenate([pair, send(pair, "gx", SWAP_HI_FAR)])


def send_near(rows):
    return send(rows[:, 256:].astype(BF16), "gx", SWAP_HI_NEAR)


def sum_columns_hi(rows, near):
    rows = rows[:, :256] + near.astype(F32)
    far = send(rows[:, 128:].astype(BF16), "gx", SWAP_HI_FAR)
    return (rows[:, :128] + far.astype(F32)).astype(BF16)


def local(tokens, gate_weight, up_weight, down_weight, out_grad):
    gx, gy, gz = lax.axis_index("gx"), lax.axis_index("gy"), lax.axis_index("gz")
    lo = gz // 4
    idx = jnp.stack([gx // 2, gx % 2, gy, gz % 4, lo]).astype(jnp.int32)
    gate_w, up_w = gate_weight.T, up_weight.T

    tok_pair = pair_hi(tokens)
    down = exchange_x(after(down_weight, tok_pair).reshape(4, 448, 256))
    tok_hi = gather_hi(tok_pair)
    tok_blocks = spread_x(tok_hi)
    grad_hi = gather_hi(pair_hi(after(out_grad, tok_pair)))
    tok_own = jnp.stack(after(tok_blocks, down, grad_hi))
    tok_other = send(tok_own, "gx", SWAP_CORE)
    grad_own = exchange_x(after(jnp.broadcast_to(grad_hi, (4, 4, 256, 128)), tok_own))
    msg = [shape((2, 448, 256), BF16)] * 3
    tok, *gu_parts = call(
        first_kernel,
        [shape((1024, 1024), BF16)] + msg,
        (idx, tok_own, tok_other, gate_w, up_w),
        (2, 3),
        (0, 1, 2, 3),
    )
    gu_received = send_y(gu_parts)
    (gu_keep,) = call(
        keep_kernel,
        [shape((2, 448, 256), F32)],
        (idx, tok, gate_w, up_w),
        (0, 1, 2),
    )
    gu_received = after(gu_received, gu_keep)
    grad_other = send(after(grad_own, gu_received), "gx", SWAP_CORE)
    msg = [shape((1, 448, 256), BF16)] * 3
    grad, down_w, dh_keep, *dh_parts = call(
        second_kernel,
        [shape((1024, 1024), BF16), shape((448, 1024), BF16), shape((1, 448, 256), F32)] + msg,
        (idx, grad_own, grad_other, down),
        (2,),
        (0, 1),
    )
    gate_up = sum_rows(gu_keep, after(gu_received, dh_parts), lo)
    dh = sum_rows(dh_keep, send_y(dh_parts), lo)[0]
    gate, up = gate_up[0], gate_up[1]
    sig = jax.nn.sigmoid(gate)
    act = gate * sig
    hidden = (act * up).astype(BF16)
    gate_delta = (dh * up * sig * (1.0 + gate * (1.0 - sig))).astype(BF16)
    up_delta = (dh * act).astype(BF16)

    hid_pair = pair_rows(hidden[None])
    hid_pieces = spread_y(hid_pair)
    delta_pair = pair_rows(after(jnp.stack([gate_delta, up_delta]), hid_pair))
    delta_pieces = spread_y(delta_pair)
    hid_pieces = after(hid_pieces, delta_pair)
    hid, mixed_other, mixed_columns = call(
        other_kernel,
        [shape((1, 448, 1024), BF16), shape((1024, 512), F32), shape((1, 448, 512), BF16)],
        (idx, *hid_pieces, down_w),
        (4,),
        (0,),
        [pltpu.VMEM((1, 448, 512), BF16)],
    )
    mixed_swapped = send(mixed_other, "gx", SWAP_CORE)
    (mixed_own,) = call(own_kernel, [shape((1024, 512), F32)], (idx, hid, mixed_columns), (0,))
    mixed_rows, mixed_parts = sum_core(mixed_own, mixed_swapped)
    mixed_received = send_x(mixed_parts)
    mixed_rows = sum_x(mixed_rows, mixed_received)
    (product,) = call(
        product_kernel,
        [shape((4, 448, 256), BF16)],
        (idx, hid, grad),
        (0, 1),
    )
    delta_pieces = after(delta_pieces, mixed_received, product)
    delta, dx_other, dx_columns = call(
        other_kernel,
        [shape((2, 448, 1024), BF16), shape((1024, 512), F32), shape((2, 448, 512), BF16)],
        (idx, *delta_pieces, gate_w, up_w),
        (4, 5),
        (0,),
        [pltpu.VMEM((2, 448, 512), BF16)],
    )
    dx_swapped = send(dx_other, "gx", SWAP_CORE)
    (dx_own,) = call(own_kernel, [shape((1024, 512), F32)], (idx, delta, dx_columns), (0,))
    dx_rows, dx_parts = sum_core(dx_own, dx_swapped)
    down_grad = exchange_x(after(product, dx_parts)).reshape(1792, 256)
    mixed_near = send_near(after(mixed_rows, dx_parts))
    dx_received = after(send_x(dx_parts), mixed_near)
    delta = after(delta, dx_parts)
    mixed = sum_columns_hi(mixed_rows, mixed_near)
    down_grad = after(down_grad, dx_received)
    dx_rows = sum_x(dx_rows, dx_received)
    tokens_grad = sum_columns_hi(dx_rows, send_near(dx_rows))

    gate_grad = jnp.dot(delta[0], tok, preferred_element_type=F32).astype(BF16).T
    up_grad = jnp.dot(after(delta[1], dx_received), tok, preferred_element_type=F32).astype(BF16).T
    return mixed, tokens_grad, gate_grad, up_grad, down_grad


def solution(mesh):
    in_specs = (
        P("gy", ("gz", "gx")),
        P("gz", ("gx", "gy")),
        P("gz", ("gx", "gy")),
        P("gx", ("gz", "gy")),
        P("gy", ("gz", "gx")),
    )
    out_specs = (
        P("gy", ("gz", "gx")),
        P("gy", ("gz", "gx")),
        P("gz", ("gx", "gy")),
        P("gz", ("gx", "gy")),
        P("gx", ("gz", "gy")),
    )
    return jax.shard_map(local, mesh=mesh, in_specs=in_specs, out_specs=out_specs, check_vma=False)
```

```python
import jax
import jax.numpy as jnp
from jax import lax
from jax.experimental import pallas as pl
from jax.experimental.pallas import tpu as pltpu
from jax.sharding import PartitionSpec as P

F32 = jnp.float32
BF16 = jnp.bfloat16
VMEM_LIMIT = 24 * 1024 * 1024


def shift_x(k):
    return [(g, (g + k) % 4) for g in range(4)]


def shift_y(k):
    return [(z * 4 + y, z * 4 + (y + k) % 4) for z in range(2) for y in range(4)]


SWAP_CORE = [(i, i ^ 1) for i in range(8)]
SWAP_LO = [(i, i ^ 4) for i in range(8)]
SWAP_HI_NEAR = [(i, i ^ 2) for i in range(8)]
SWAP_HI_FAR = [(i, i ^ 6) for i in range(8)]


def send(value, axis, moves):
    return lax.ppermute(value, axis, moves)


def staged(kernel, n_in, outs, far, n_scratch):
    n_out = len(outs)

    def run(idx, *refs):
        inputs, results = refs[:n_in], refs[n_in : n_in + n_out]
        scratch = refs[n_in + n_out : n_in + n_out + n_scratch]
        held = refs[n_in + n_out + n_scratch : -1]
        held, near, sems = held[:n_in], held[n_in:], refs[-1]
        copies = [
            pltpu.make_async_copy(src, dst, sems.at[i])
            for i, (src, dst) in enumerate(zip(inputs, held))
        ]
        for copy in copies:
            copy.start()
        for copy in copies:
            copy.wait()
        local_results = list(results)
        for i, ref in zip(far, near):
            local_results[i] = ref
        leaving = {
            i: pltpu.make_async_copy(ref, results[i], sems.at[n_in + n])
            for n, (i, ref) in enumerate(zip(far, near))
        }
        kernel(lambda i: leaving[i].start(), idx, *held, *local_results, *scratch)
        for i in far:
            leaving[i].wait()

    return run


def call(kernel, outs, args, far_in=(), far=(), scratch=()):
    n = len(args) - 1
    return pl.pallas_call(
        staged(kernel, n, outs, far, len(scratch)),
        out_shape=[
            pltpu.HBM(o.shape, o.dtype) if i in far else o for i, o in enumerate(outs)
        ],
        in_specs=[pl.BlockSpec(memory_space=pltpu.SMEM)]
        + [pl.BlockSpec(memory_space=pltpu.HBM if i in far_in else pl.ANY) for i in range(n)],
        out_specs=[
            pl.BlockSpec(memory_space=pltpu.HBM if i in far else pltpu.VMEM)
            for i in range(len(outs))
        ],
        scratch_shapes=list(scratch)
        + [pltpu.VMEM(a.shape, a.dtype) for a in args[1:]]
        + [pltpu.VMEM(outs[i].shape, outs[i].dtype) for i in far]
        + [pltpu.SemaphoreType.DMA((n + len(far),))],
        compiler_params=pltpu.CompilerParams(vmem_limit_bytes=VMEM_LIMIT),
        cost_estimate=pl.CostEstimate(flops=1, bytes_accessed=1, transcendentals=0),
    )(
        args[0],
        *[
            pltpu.with_memory_space_constraint(a, pltpu.HBM) if i in far_in else a
            for i, a in enumerate(args[1:])
        ],
    )


def shape(dims, dtype):
    return jax.ShapeDtypeStruct(dims, dtype)


def dot_nt(left, right):
    return lax.dot_general(left, right, (((1,), (1,)), ((), ())), preferred_element_type=F32)


def dot_tn(left, right):
    return lax.dot_general(left, right, (((0,), (0,)), ((), ())), preferred_element_type=F32)


def rows_of(start, size):
    return pl.ds(pl.multiple_of(start, size), size)


GATHERED = (0, 1, 3, 2)
SCATTERED = (0, 3, 1, 2)


def place_activation(hi, core, own_ref, other_ref, act_ref, order):
    for slot, mask in enumerate(GATHERED):
        block = (hi ^ mask) * 2
        for x in range(4):
            rows = slice(x * 256, (x + 1) * 256)
            act_ref[rows, rows_of((block + core) * 128, 128)] = own_ref[order[x], slot]
            act_ref[rows, rows_of((block + 1 - core) * 128, 128)] = other_ref[order[x], slot]


def partials(y, weights, act_ref, sends, sent):
    for k in (2, 1, 3):
        act = act_ref[rows_of(lax.rem(y + k, 4) * 256, 256), :]
        for i, w_ref in enumerate(weights):
            sends[k - 1][i] = dot_nt(w_ref[...], act).astype(BF16)
        sent(k)


def kept(y, weights, act_ref, keep_ref):
    act = act_ref[rows_of(y * 256, 256), :]
    for i, w_ref in enumerate(weights):
        keep_ref[i] = dot_nt(w_ref[...], act)


def first_kernel(flush, idx, own, other, gate_w, up_w, act, s1, s2, s3):
    place_activation(idx[0], idx[1], own, other, act, range(4))
    flush(0)
    partials(idx[3], (gate_w, up_w), act, (s1, s2, s3), flush)


def keep_kernel(flush, idx, act, gate_w, up_w, keep):
    kept(idx[3], (gate_w, up_w), act, keep)


def second_kernel(flush, idx, own, other, down, act, weight, keep, s1, s2, s3):
    for x in range(4):
        weight[:, x * 256 : (x + 1) * 256] = down[x]
    order = [lax.rem(idx[2] + 4 - k, 4) for k in range(4)]
    flush(1)
    place_activation(idx[0], idx[1], own, other, act, order)
    flush(0)
    partials(idx[3], (weight,), act, (s1, s2, s3), lambda k: None)
    kept(idx[3], (weight,), act, keep)


def place_hidden(idx, n, pieces, whole):
    y, lo = idx[3], idx[4]
    for k, piece in enumerate(pieces):
        start = lax.rem(y + 4 - k, 4) * 256
        for j, half in ((0, lo), (1, 1 - lo)):
            for i in range(n):
                whole[i, :, rows_of(start + half * 128, 128)] = piece[j, i]


def place_columns(idx, core, weights, columns):
    for i, w in enumerate(weights):
        for k, mask in enumerate(SCATTERED):
            block = (idx[0] ^ mask) * 2 + core
            columns[i, :, k * 128 : (k + 1) * 128] = w[:, rows_of(block * 128, 128)]


def back_product(n, whole, columns, out):
    for t in range(4):
        rows = slice(t * 256, (t + 1) * 256)
        total = dot_tn(whole[0, :, rows], columns[0])
        for i in range(1, n):
            total = total + dot_tn(whole[i, :, rows], columns[i])
        out[rows, :] = total


def other_kernel(flush, idx, p0, p1, p2, p3, *refs):
    weights, (whole, other, mine, theirs) = refs[:-4], refs[-4:]
    n = len(weights)
    place_hidden(idx, n, (p0, p1, p2, p3), whole)
    flush(0)
    place_columns(idx, 1 - idx[1], weights, theirs)
    back_product(n, whole, theirs, other)
    place_columns(idx, idx[1], weights, mine)


def own_kernel(flush, idx, whole, columns, own):
    back_product(whole.shape[0], whole, columns, own)


def product_kernel(flush, idx, hid, grad, out):
    for x in range(4):
        part = jnp.dot(hid[0], grad[:, x * 256 : (x + 1) * 256], preferred_element_type=F32)
        out[x] = part.astype(BF16)


def exchange_x(blocks):
    return lax.all_to_all(blocks, "gy", split_axis=0, concat_axis=0, tiled=True)


def together(values):
    return list(lax.optimization_barrier(tuple(values)))


def after(value, *others):
    return lax.optimization_barrier((value, others))[0]


def spread_x(block):
    return [block] + together([send(block, "gy", shift_x(k)) for k in (1, 2, 3)])


def send_y(parts):
    return together([send(part, "gz", shift_y(k)) for k, part in zip((1, 2, 3), parts)])


def sum_rows(keep, received, lo):
    total = keep
    for part in received:
        total = total + part.astype(F32)
    low, high = total[..., :128], total[..., 128:]
    mine = jnp.where(lo == 0, low, high)
    theirs = jnp.where(lo == 0, high, low)
    return mine + send(theirs, "gz", SWAP_LO)


def pair_rows(block):
    return jnp.stack([block, send(block, "gz", SWAP_LO)])


def spread_y(pair):
    return [pair] + together([send(pair, "gz", shift_y(k)) for k in (1, 2, 3)])


def sum_core(own, swapped):
    total = own + swapped
    return total[:256], [total[k * 256 : (k + 1) * 256].astype(BF16) for k in (1, 2, 3)]


def send_x(parts):
    return together([send(part, "gy", shift_x(-k)) for k, part in zip((1, 2, 3), parts)])


def sum_x(rows, received):
    for part in received:
        rows = rows + part.astype(F32)
    return rows


def pair_hi(block):
    return jnp.stack([block, send(block, "gx", SWAP_HI_NEAR)])


def gather_hi(pair):
    return jnp.concatenate([pair, send(pair, "gx", SWAP_HI_FAR)])


def send_near(rows):
    return send(rows[:, 256:].astype(BF16), "gx", SWAP_HI_NEAR)


def sum_columns_hi(rows, near):
    rows = rows[:, :256] + near.astype(F32)
    far = send(rows[:, 128:].astype(BF16), "gx", SWAP_HI_FAR)
    return (rows[:, :128] + far.astype(F32)).astype(BF16)


def local(tokens, gate_weight, up_weight, down_weight, out_grad):
    gx, gy, gz = lax.axis_index("gx"), lax.axis_index("gy"), lax.axis_index("gz")
    lo = gz // 4
    idx = jnp.stack([gx // 2, gx % 2, gy, gz % 4, lo]).astype(jnp.int32)
    gate_w, up_w = gate_weight.T, up_weight.T

    tok_pair = pair_hi(tokens)
    down = exchange_x(after(down_weight, tok_pair).reshape(4, 448, 256))
    tok_hi = gather_hi(tok_pair)
    tok_blocks = spread_x(tok_hi)
    grad_hi = gather_hi(pair_hi(after(out_grad, tok_pair)))
    tok_own = jnp.stack(after(tok_blocks, down, grad_hi))
    tok_other = send(tok_own, "gx", SWAP_CORE)
    grad_own = exchange_x(after(jnp.broadcast_to(grad_hi, (4, 4, 256, 128)), tok_own))
    msg = [shape((2, 448, 256), BF16)] * 3
    tok, *gu_parts = call(
        first_kernel,
        [shape((1024, 1024), BF16)] + msg,
        (idx, tok_own, tok_other, gate_w, up_w),
        (2, 3),
        (0, 1, 2, 3),
    )
    gu_received = send_y(gu_parts)
    (gu_keep,) = call(
        keep_kernel,
        [shape((2, 448, 256), F32)],
        (idx, tok, gate_w, up_w),
        (0, 1, 2),
    )
    gu_received = after(gu_received, gu_keep)
    grad_other = send(after(grad_own, gu_received), "gx", SWAP_CORE)
    msg = [shape((1, 448, 256), BF16)] * 3
    grad, down_w, dh_keep, *dh_parts = call(
        second_kernel,
        [shape((1024, 1024), BF16), shape((448, 1024), BF16), shape((1, 448, 256), F32)] + msg,
        (idx, grad_own, grad_other, down),
        (2,),
        (0, 1),
    )
    gate_up = sum_rows(gu_keep, gu_received, lo)
    dh = sum_rows(dh_keep, send_y(dh_parts), lo)[0]
    gate, up = gate_up[0], gate_up[1]
    sig = jax.nn.sigmoid(gate)
    act = gate * sig
    hidden = (act * up).astype(BF16)
    gate_delta = (dh * up * sig * (1.0 + gate * (1.0 - sig))).astype(BF16)
    up_delta = (dh * act).astype(BF16)

    hid_pair = pair_rows(hidden[None])
    hid_pieces = spread_y(hid_pair)
    delta_pair = pair_rows(after(jnp.stack([gate_delta, up_delta]), hid_pair))
    delta_pieces = spread_y(delta_pair)
    hid_pieces = after(hid_pieces, delta_pair)
    hid, mixed_other, mixed_columns = call(
        other_kernel,
        [shape((1, 448, 1024), BF16), shape((1024, 512), F32), shape((1, 448, 512), BF16)],
        (idx, *hid_pieces, down_w),
        (4,),
        (0,),
        [pltpu.VMEM((1, 448, 512), BF16)],
    )
    mixed_swapped = send(mixed_other, "gx", SWAP_CORE)
    (mixed_own,) = call(own_kernel, [shape((1024, 512), F32)], (idx, hid, mixed_columns), (0,))
    mixed_rows, mixed_parts = sum_core(mixed_own, mixed_swapped)
    mixed_received = send_x(mixed_parts)
    mixed_rows = sum_x(mixed_rows, mixed_received)
    (product,) = call(
        product_kernel,
        [shape((4, 448, 256), BF16)],
        (idx, hid, grad),
        (0, 1),
    )
    delta_pieces = after(delta_pieces, mixed_received, product)
    delta, dx_other, dx_columns = call(
        other_kernel,
        [shape((2, 448, 1024), BF16), shape((1024, 512), F32), shape((2, 448, 512), BF16)],
        (idx, *delta_pieces, gate_w, up_w),
        (4, 5),
        (0,),
        [pltpu.VMEM((2, 448, 512), BF16)],
    )
    dx_swapped = send(dx_other, "gx", SWAP_CORE)
    (dx_own,) = call(own_kernel, [shape((1024, 512), F32)], (idx, delta, dx_columns), (0,))
    dx_rows, dx_parts = sum_core(dx_own, dx_swapped)
    down_grad = exchange_x(after(product, dx_parts)).reshape(1792, 256)
    mixed_near = send_near(after(mixed_rows, dx_parts))
    dx_received = after(send_x(dx_parts), mixed_near)
    delta = after(delta, dx_parts)
    mixed = sum_columns_hi(mixed_rows, mixed_near)
    down_grad = after(down_grad, dx_received)
    dx_rows = sum_x(dx_rows, dx_received)
    tokens_grad = sum_columns_hi(dx_rows, send_near(dx_rows))

    gate_grad = jnp.dot(delta[0], tok, preferred_element_type=F32).astype(BF16).T
    up_grad = jnp.dot(after(delta[1], dx_received), tok, preferred_element_type=F32).astype(BF16).T
    return mixed, tokens_grad, gate_grad, up_grad, down_grad


def solution(mesh):
    in_specs = (
        P("gy", ("gz", "gx")),
        P("gz", ("gx", "gy")),
        P("gz", ("gx", "gy")),
        P("gx", ("gz", "gy")),
        P("gy", ("gz", "gx")),
    )
    out_specs = (
        P("gy", ("gz", "gx")),
        P("gy", ("gz", "gx")),
        P("gz", ("gx", "gy")),
        P("gz", ("gx", "gy")),
        P("gx", ("gz", "gy")),
    )
    return jax.shard_map(local, mesh=mesh, in_specs=in_specs, out_specs=out_specs, check_vma=False)
```
